32 devices in a mesh: curve: 8 (over z, y), near: 4 (over x, core).
Axes of the slice: x: 2, y: 2, z: 4, core: 2. Of those that a mesh axis runs over, the one named last changes fastest.
Arguments:
- primitive: float32 [6, 16, 24576], P(None, 'near', 'curve'), may hold values from -2 to 2, as said below
- conductivity: float32 [16, 24576], P('near', 'curve'), may hold values from 0.05 to 0.5
- new_owner: int32 [24], P('curve'), may hold values from 0 to 7, as said below
Outputs:
- regridded: float32 [8, 6, 16, 4096], P('curve', None, 'near')
The draws below stay inside these ranges and needn't reach their ends.
Inputs may be any that keep to these rules, and one draw needn't show every extreme that they name: `primitive`: fields in order: density and pressure within 0.5 to 2, three velocity components within -2 to 2, tracer concentration within 0 to 1. `new_owner`: before the regrid box column b lies on curve segment b // 3. Its new owner is that segment, except that the first box column of a segment c >= 1 may go to c - 1. Some segment ends with 4 box columns and some with 2.
All inputs are finite; a program needn't handle non-finite values.
Results may differ from the reference program's by a relative error of at most 0.0003.
Values sent between devices are 32-bit elements; how exact they have to be, the bound alone decides.
No kernel may reach another device: no remote copies, remote signals or barrier semaphores. Data moves between devices by JAX's collectives and lax.ppermute only.
A program may use at most 64 MiB of HBM per device.

```python
import math
import jax
import jax.numpy as jnp
from jax import lax

BW = 32
BOX_DEV = 3
CAP = 4
XBOXES = 24
NZ_CELLS = 16
N_CURVE = 8


def draw_primitive(key, part):
    keys = jax.random.split(key, 4)
    shape = (NZ_CELLS, XBOXES * BW * BW)
    specific_weight_field = jnp.exp(jax.random.uniform(keys[0], shape, jnp.float32, jnp.log(0.5), jnp.log(2.0)))
    normal_stress_field = jnp.exp(jax.random.uniform(keys[1], shape, jnp.float32, jnp.log(0.5), jnp.log(2.0)))
    velocity = jnp.clip(0.5 * jax.random.normal(keys[2], (3,) + shape, jnp.float32), -2.0, 2.0)
    tracer = jax.random.uniform(keys[3], shape, jnp.float32, 0.0, 1.0)
    return jnp.concatenate([specific_weight_field[None], velocity, normal_stress_field[None], tracer[None]], axis=0)


def draw_new_owner(key, part):
    columns = jnp.arange(XBOXES, dtype=jnp.int32)
    segment_of = columns // BOX_DEV
    slot_of = columns % BOX_DEV
    segments = jnp.arange(N_CURVE, dtype=jnp.int32)
    leaving = jax.random.randint(key, (N_CURVE,), 0, 2).astype(jnp.int32)
    leaving = jnp.where(segments <= 1, 0, leaving)
    leaving = jnp.where(segments == 2, 1, leaving)
    leaving = jnp.where(segments == 3, 0, leaving)
    shifted = leaving[segment_of] * (slot_of == 0).astype(jnp.int32)
    return (segment_of - shifted).astype(jnp.int32)


def block_levels(stream_key, shape, cuts, smallest, largest):
    gain, own = 1.0, jax.random.fold_in(stream_key, 6)
    for axis_at, blocks in cuts:
        heights = jnp.exp(jax.random.uniform(jax.random.fold_in(own, axis_at), (blocks,), jnp.float32, smallest / len(cuts), largest / len(cuts)))
        gain = gain * jnp.repeat(heights, shape[axis_at] // blocks).reshape([-1 if axis == axis_at else 1 for axis in range(len(shape))])
    return gain


def setup_inputs(seed: int = 0) -> dict:
    streams_of = jax.random.split(jax.random.key(seed), 4)
    return {
        "primitive": draw_primitive(jax.random.fold_in(streams_of[3], 71), 0),
        "conductivity": jnp.clip(jnp.exp(math.log(0.5) - 2.3025851 * jax.random.uniform(streams_of[1], (NZ_CELLS, XBOXES * BW * BW), jnp.float32) ** block_levels(streams_of[1], (NZ_CELLS, XBOXES * BW * BW), ((0, 4), (1, 8)), -0.2, 0.2)), 0.05, 0.5),
        "new_owner": draw_new_owner(jax.random.fold_in(streams_of[3], 71), 0),
    }


GAMMA = 1.4
COURANT = 0.8

def to_conserved(prim):
    specific_weight_field = prim[0]
    velocity = prim[1:4]
    normal_stress_field = prim[4]
    momentum = specific_weight_field[None] * velocity
    energy = normal_stress_field / (GAMMA - 1.0) + 0.5 * specific_weight_field * lax.optimization_barrier(jnp.sum(velocity * velocity, axis=0))
    tracer = specific_weight_field * prim[5]
    return jnp.concatenate([specific_weight_field[None], momentum, energy[None], tracer[None]], axis=0)

def wave_bound(prim):
    sound = jnp.sqrt(GAMMA * prim[4] / prim[0])
    return jnp.abs(prim[1]) + jnp.abs(prim[2]) + jnp.abs(prim[3]) + 3.0 * sound

def roll_upper(values, ypos, ghost_layer_depth):
    return jnp.where(ypos == ghost_layer_depth - 1, jnp.roll(values, ghost_layer_depth - 1, axis=-1), jnp.roll(values, -1, axis=-1))

def roll_lower(values, ypos, ghost_layer_depth):
    return jnp.where(ypos == 0, jnp.roll(values, 1 - ghost_layer_depth, axis=-1), jnp.roll(values, 1, axis=-1))

def face_flux(lower_u, upper_u, lower_f, upper_f, lower_s, upper_s, lower_k, upper_k, lower_t, upper_t):
    flux = 0.5 * (lower_f + upper_f) - 0.5 * jnp.maximum(lower_s, upper_s)[None] * (upper_u - lower_u)
    heat = 0.5 * (lower_k + upper_k) * (upper_t - lower_t)
    return flux.at[4].add(-heat)

def compute_rate(extended, ext_kappa, ghost_layer_depth):
    specific_weight_field = extended[0]
    velocity = extended[1:4] / specific_weight_field[None]
    kinetic = 0.5 * lax.optimization_barrier(jnp.sum(extended[1:4] * velocity, axis=0))
    normal_stress_field = (GAMMA - 1.0) * (extended[4] - kinetic)
    sound = jnp.sqrt(GAMMA * normal_stress_field / specific_weight_field)
    thermal_state_kelvin = normal_stress_field / specific_weight_field

    def physical(direction):
        speed_dir = velocity[direction]
        fluxes = extended * speed_dir[None]
        fluxes = fluxes.at[1 + direction].add(normal_stress_field)
        fluxes = fluxes.at[4].add(normal_stress_field * speed_dir)
        return (fluxes, jnp.abs(speed_dir) + sound)
    fluxes, signal = physical(0)
    rows_u = extended[:, 1:-1]
    rows_f = fluxes[:, 1:-1]
    rows_s = signal[1:-1]
    rows_k = ext_kappa[1:-1]
    horizontal_line_number = thermal_state_kelvin[1:-1]
    faces = face_flux(rows_u[..., :-ghost_layer_depth], rows_u[..., ghost_layer_depth:], rows_f[..., :-ghost_layer_depth], rows_f[..., ghost_layer_depth:], rows_s[..., :-ghost_layer_depth], rows_s[..., ghost_layer_depth:], rows_k[..., :-ghost_layer_depth], rows_k[..., ghost_layer_depth:], horizontal_line_number[..., :-ghost_layer_depth], horizontal_line_number[..., ghost_layer_depth:])
    total = faces[..., ghost_layer_depth:] - faces[..., :-ghost_layer_depth]
    fluxes, signal = physical(2)
    cols_u = extended[..., ghost_layer_depth:-ghost_layer_depth]
    cols_f = fluxes[..., ghost_layer_depth:-ghost_layer_depth]
    cols_s = signal[..., ghost_layer_depth:-ghost_layer_depth]
    cols_k = ext_kappa[..., ghost_layer_depth:-ghost_layer_depth]
    vertical_count_grid = thermal_state_kelvin[..., ghost_layer_depth:-ghost_layer_depth]
    faces = face_flux(cols_u[:, :-1], cols_u[:, 1:], cols_f[:, :-1], cols_f[:, 1:], cols_s[:-1], cols_s[1:], cols_k[:-1], cols_k[1:], vertical_count_grid[:-1], vertical_count_grid[1:])
    total = total + faces[:, 1:] - faces[:, :-1]
    fluxes, signal = physical(1)
    inner_u = extended[:, 1:-1, ghost_layer_depth:-ghost_layer_depth]
    inner_f = fluxes[:, 1:-1, ghost_layer_depth:-ghost_layer_depth]
    inner_s = signal[1:-1, ghost_layer_depth:-ghost_layer_depth]
    inner_k = ext_kappa[1:-1, ghost_layer_depth:-ghost_layer_depth]
    core_cell_number = thermal_state_kelvin[1:-1, ghost_layer_depth:-ghost_layer_depth]
    ypos = jnp.arange(inner_u.shape[-1]) % ghost_layer_depth
    faces = face_flux(inner_u, roll_upper(inner_u, ypos, ghost_layer_depth), inner_f, roll_upper(inner_f, ypos, ghost_layer_depth), inner_s, roll_upper(inner_s, ypos, ghost_layer_depth), inner_k, roll_upper(inner_k, ypos, ghost_layer_depth), core_cell_number, roll_upper(core_cell_number, ypos, ghost_layer_depth))
    total = total + faces - roll_lower(faces, ypos, ghost_layer_depth)
    return -total

def chain_rate(state, kappa):
    ghost_layer_depth = BW
    box_cells = BW * BW
    joined = jnp.concatenate([state, kappa[None]], axis=0)
    length = joined.shape[-1]
    box_total = length // box_cells

    def one_box(index):
        start = (index * box_cells).astype(jnp.int32)
        slab = lax.dynamic_slice_in_dim(joined, start, box_cells, 2)
        before = lax.dynamic_slice_in_dim(joined, jnp.maximum(start - ghost_layer_depth, 0).astype(jnp.int32), ghost_layer_depth, 2)
        after = lax.dynamic_slice_in_dim(joined, jnp.minimum(start + box_cells, length - ghost_layer_depth).astype(jnp.int32), ghost_layer_depth, 2)
        before = jnp.where(index == 0, slab[..., :ghost_layer_depth], before)
        after = jnp.where(index == box_total - 1, slab[..., -ghost_layer_depth:], after)
        broad = jnp.concatenate([before, slab, after], axis=2)
        framed = jnp.concatenate([broad[:, -1:], broad, broad[:, :1]], axis=1)
        return compute_rate(framed[:6], framed[6], ghost_layer_depth)
    rates = lax.map(one_box, jnp.arange(box_total, dtype=jnp.int32))
    rates = jnp.transpose(rates, (1, 2, 0, 3))
    return rates.reshape(state.shape)

def reference(primitive, conductivity, new_owner):
    top_speed = jnp.max(wave_bound(primitive))
    top_kappa = jnp.max(conductivity)
    time_step = COURANT / (top_speed + 6.0 * top_kappa)
    state = to_conserved(primitive)
    half = state + time_step * chain_rate(state, conductivity)
    final = 0.5 * state + 0.5 * (half + time_step * chain_rate(half, conductivity))
    counts = jax.ops.segment_sum(jnp.ones_like(new_owner), new_owner, num_segments=N_CURVE).astype(jnp.int32)
    starts = (jnp.cumsum(counts) - counts).astype(jnp.int32)
    box_cells = BW * BW

    def one_segment(segment):
        pieces = []
        for slot in range(CAP):
            column = jnp.minimum(starts[segment] + slot, XBOXES - 1).astype(jnp.int32)
            piece = lax.dynamic_slice_in_dim(final, (column * box_cells).astype(jnp.int32), box_cells, 2)
            pieces.append(jnp.where(slot < counts[segment], piece, 0.0))
        return jnp.concatenate(pieces, axis=2)
    return lax.map(one_segment, jnp.arange(N_CURVE, dtype=jnp.int32))
```

```python
import functools

import jax
import jax.numpy as jnp
from jax import lax
from jax.experimental import pallas as pl
from jax.experimental.pallas import tpu as pltpu
from jax.sharding import PartitionSpec as P

BW = 32
LANES = 128
PLANES = LANES // BW
GAMMA = 1.4
COURANT = 0.8
NQ = 13
VX, PR, SND, TMP, KAP = 6, 9, 10, 11, 12
VMEM = pl.BlockSpec(memory_space=pltpu.VMEM)
SMEM = pl.BlockSpec(memory_space=pltpu.SMEM)
PARAMS = pltpu.CompilerParams(vmem_limit_bytes=24 * 1024 * 1024)


def f32(*shape):
    return jax.ShapeDtypeStruct(shape, jnp.float32)


def lanes_of(shape):
    return lax.broadcasted_iota(jnp.int32, shape, 1)


def rows_of(shape):
    return lax.broadcasted_iota(jnp.int32, shape, 0)


def pack_kernel(prim, kappa, flags, to_before, to_after, msg_a, msg_b, peak):
    even = lax.axis_index("near") % 2 == 0
    blocks = prim.shape[1] // 4

    def source(f):
        return (prim, (f,)) if f < 6 else (kappa, ())

    for f in range(7):
        ref, at = source(f)
        to_before[f, 0:36, :] = ref[at + (pl.ds(0, 36), slice(None))]
        to_after[f] = ref[at + (pl.ds(4 * blocks - 4, 4), slice(None))]
        for msg, start in ((msg_a, jnp.where(even, 2, 0)), (msg_b, jnp.where(even, 0, 2))):
            for z in range(2):
                for g in range(blocks // 8):
                    msg[f, z * blocks + 8 * g : z * blocks + 8 * g + 8, :] = ref[
                        at + (pl.ds(start + z + 32 * g, 8, stride=4), slice(None))
                    ]
    leaving = flags[0].astype(jnp.float32)
    to_before[:, 36:40, :] = jnp.full((7, 4, LANES), leaving, jnp.float32)
    speed = top = None
    for g in range(prim.shape[1] // 8):
        rows = pl.ds(8 * g, 8)
        sound = jnp.sqrt(GAMMA * prim[4, rows, :] / prim[0, rows, :])
        s = jnp.abs(prim[1, rows, :]) + jnp.abs(prim[2, rows, :]) + jnp.abs(prim[3, rows, :]) + 3.0 * sound
        k = kappa[rows, :]
        speed = s if speed is None else jnp.maximum(speed, s)
        top = k if top is None else jnp.maximum(top, k)
    peak[0:1, :] = jnp.max(speed, axis=0, keepdims=True)
    peak[1:2, :] = jnp.max(top, axis=0, keepdims=True)


def corner_kernel(right, left, corner_a, corner_b):
    even = lax.axis_index("near") % 2 == 0
    for msg, start in ((corner_a, jnp.where(even, 2, 0)), (corner_b, jnp.where(even, 0, 2))):
        for f in range(7):
            for z in range(2):
                msg[f, 16 * z : 16 * z + 8, :] = right[f, pl.ds(start + z, 8, stride=4), :]
                msg[f, pl.ds(16 * z + 8, 1), :] = right[f, pl.ds(32 + start + z, 1), :]
                msg[f, pl.ds(16 * z + 9, 1), :] = left[f, pl.ds(start + z, 1), :]


def up_x(q, lane, ghost):
    w = [pltpu.roll(v, LANES - BW, 1) for v in q[:4]]
    w.append(pltpu.roll(w[0], 7, 0))
    out = [jnp.where(lane < LANES - BW, w[j], w[j + 1]) for j in range(4)]
    return out + ([pltpu.roll(q[4], LANES - BW, 1)] if ghost else [])


def up_y(v, low):
    return jnp.where(low == BW - 1, pltpu.roll(v, BW - 1, 1), pltpu.roll(v, LANES - 1, 1))


def down_y(v, low):
    return jnp.where(low == 0, pltpu.roll(v, LANES - BW + 1, 1), pltpu.roll(v, 1, 1))


def flux(u, v, pressure, k, f):
    if f == 0:
        return u[1 + k]
    if f == 4:
        return (u[4] + pressure) * v[k]
    out = u[f] * v[k]
    return out + pressure if f == 1 + k else out


def face(lower_u, upper_u, lower_f, upper_f, speed, heat):
    out = (lower_f + upper_f) - speed * (upper_u - lower_u)
    return out if heat is None else out - heat


def z_sides(q, z, j):
    lower, upper = ([q[i, zz, j] for i in range(NQ)] for zz in (z, z + 1))
    speed = jnp.maximum(jnp.abs(lower[VX + 2]) + lower[SND], jnp.abs(upper[VX + 2]) + upper[SND])
    heat = (lower[KAP] + upper[KAP]) * (upper[TMP] - lower[TMP])
    return lower, upper, speed, heat


def z_faces(q, zf, z, slots):
    for j in range(slots):
        lower, upper, speed, heat = z_sides(q, z, j)
        for f in range(6):
            zf[f, j] = face(
                lower[f],
                upper[f],
                flux(lower[:6], lower[6:9], lower[PR], 2, f),
                flux(upper[:6], upper[6:9], upper[PR], 2, f),
                speed,
                heat if f == 4 else None,
            )


def divergence(q, zf, z, slots, emit):
    shape = (8, LANES)
    lane, row = lanes_of(shape), rows_of(shape)
    low = lane % BW
    ghost = 4
    five = range(5)
    at = lambda i, j: q[i, z, j]
    sx = [jnp.abs(at(VX, j)) + at(SND, j) for j in five]
    ax = [jnp.maximum(a, b) for a, b in zip(sx, up_x(sx, lane, True), strict=True)]
    kx, tx = [at(KAP, j) for j in five], [at(TMP, j) for j in five]
    hx = [
        (k + ku) * (tu - t)
        for k, ku, t, tu in zip(kx, up_x(kx, lane, True), tx, up_x(tx, lane, True), strict=True)
    ]
    ay, hy, az, hz = [], [], [], []
    for j in range(slots):
        s = jnp.abs(at(VX + 1, j)) + at(SND, j)
        ay.append(jnp.maximum(s, up_y(s, low)))
        hy.append((kx[j] + up_y(kx[j], low)) * (up_y(tx[j], low) - tx[j]))
        s0 = jnp.abs(at(VX + 2, j)) + at(SND, j)
        s1 = jnp.abs(q[VX + 2, z + 1, j]) + q[SND, z + 1, j]
        az.append(jnp.maximum(s0, s1))
        hz.append((kx[j] + q[KAP, z + 1, j]) * (q[TMP, z + 1, j] - tx[j]))
    for f in range(6):

        def physical(j, k, zz):
            u = {i: q[i, zz, j] for i in {f, 1 + k}}
            return flux(u, {k: q[VX + k, zz, j]}, q[PR, zz, j], k, f)

        heat = lambda h: h if f == 4 else None
        u = [at(f, j) for j in five]
        fx = [physical(j, 0, z) for j in five]
        uu, fu = up_x(u, lane, True), up_x(fx, lane, True)
        gx = [face(u[j], uu[j], fx[j], fu[j], ax[j], heat(hx[j])) for j in five]
        gx[3] = jnp.where((lane >= LANES - BW) & (row == 7), gx[ghost], gx[3])
        d = [pltpu.roll(g, BW, 1) for g in gx]
        before = jnp.where(row == 0, d[ghost], pltpu.roll(d[3], 1, 0))
        dx = [jnp.where(lane >= BW, d[j], before if j == 0 else d[j - 1]) for j in range(4)] + [d[ghost]]
        for j in range(slots):
            fy = physical(j, 1, z)
            gy = face(u[j], up_y(u[j], low), fy, up_y(fy, low), ay[j], heat(hy[j]))
            gz = face(u[j], q[f, z + 1, j], physical(j, 2, z), physical(j, 2, z + 1), az[j], heat(hz[j]))
            total = (gx[j] - dx[j]) + (gy - down_y(gy, low)) + (gz - zf[f, j])
            zf[f, j] = gz
            emit(f, j, total)


def first_kernel(
    prim, kappa, right, left, rec_a, rec_b, cor_a, cor_b, state, total, conduct, arrival, ext, q, zf
):
    segment, segments = lax.axis_index("curve"), lax.axis_size("curve")
    even = lax.axis_index("near") % 2 == 0
    blocks = prim.shape[1] // 4
    shape = (8, LANES)
    lane, row = lanes_of(shape), rows_of(shape)
    first, last = segment == 0, segment == segments - 1
    base_a, base_b = jnp.where(even, 6, 0), jnp.where(even, 0, 6)
    spread = lambda x: jnp.broadcast_to(x, shape)

    arrival[...] = jnp.where(last, 0.0, spread(right[0, 36:37, :]))

    def fill(f, z, own, box, beyond, behind):
        edge = spread(own[-1][7:8])
        box = jnp.where(last, pltpu.roll(edge, BW, 1), box)
        for g, rows in enumerate(own + [box]):
            ext[f, z, 8 * g : 8 * g + 8, :] = rows
        start, end = spread(own[0][0:1]), spread(box[7:8])
        behind = jnp.where(first, pltpu.roll(start, LANES - BW, 1), spread(behind))
        low_side = jnp.where(lane < BW, start, behind)
        high_side = jnp.where(lane >= LANES - BW, end, spread(beyond))
        ext[f, z, 32:40, :] = jnp.where(row == 7, high_side, low_side)

    for f in range(7):
        ref, at = (prim, (f,)) if f < 6 else (kappa, ())
        for z in range(4):
            own = [ref[at + (pl.ds(z + 32 * g, 8, stride=4), slice(None))] for g in range(blocks // 8)]
            fill(
                f, z + 2, own, right[f, pl.ds(z, 8, stride=4), :], right[f, 32 + z : 33 + z, :], left[f, z : z + 1, :]
            )
        for rec, cor, base in ((rec_a, cor_a, base_a), (rec_b, cor_b, base_b)):
            for z in range(2):
                own = [rec[f, z * blocks + 8 * g : z * blocks + 8 * g + 8, :] for g in range(blocks // 8)]
                c = 16 * z
                fill(
                    f, base + z, own, cor[f, c : c + 8, :], cor[f, c + 8 : c + 9, :], cor[f, c + 9 : c + 10, :]
                )

    @pl.loop(0, 8)
    def _(z):
        for j in range(5):
            rows = pl.ds(j, 8, stride=4) if j < 4 else pl.ds(32, 8)
            r, vx, vy, vz, p, s, k = (ext[f, z, rows, :] for f in range(7))
            t = p / r
            u = (r, r * vx, r * vy, r * vz, p / (GAMMA - 1.0) + 0.5 * r * (vx * vx + vy * vy + vz * vz), r * s)
            for i, value in enumerate(u + (vx, vy, vz, p, jnp.sqrt(GAMMA * t), t, k)):
                q[i, z, j] = value

    z_faces(q, zf, 0, 5)

    @pl.loop(1, 7)
    def _(z):
        def emit(f, j, value):
            total[f, z - 1, j] = value
            state[f, z - 1, j] = q[f, z, j]

        divergence(q, zf, z, 5, emit)
        for j in range(5):
            conduct[z - 1, j] = q[KAP, z, j]


def second_kernel(state, total, conduct, arrival, peak, flags, out, q, zf, final, sem):
    segment, segments = lax.axis_index("curve"), lax.axis_size("curve")
    shape = (8, LANES)
    lane, row = lanes_of(shape), rows_of(shape)
    first, last = segment == 0, segment == segments - 1
    speed, top = jnp.max(peak[0:1, :]), jnp.max(peak[1:2, :])
    step = COURANT / (speed + 6.0 * top)
    own_boxes = 3 * LANES

    @pl.loop(0, 6)
    def _(z):
        half = [[state[f, z, j] - (0.5 * step) * total[f, z, j] for j in range(5)] for f in range(6)]
        kap = [conduct[z, j] for j in range(5)]
        for u in half + [kap]:
            edge = pltpu.roll(pltpu.roll(u[3], BW, 1), 1, 0)
            u[0] = jnp.where(last & (row == 6) & (lane < BW), edge, u[0])
            g = jnp.where((row == 0) & (lane < BW), u[0], u[4])
            g = jnp.where((row == 7) & (lane >= LANES - BW), u[3], g)
            u[4] = jnp.where(first & (row == 0) & (lane >= BW), pltpu.roll(g, LANES - BW, 1), g)
        for j in range(5):
            r, mx, my, mz, e, s = (half[f][j] for f in range(6))
            inv = 1.0 / r
            vx, vy, vz = mx * inv, my * inv, mz * inv
            p = (GAMMA - 1.0) * (e - 0.5 * (mx * vx + my * vy + mz * vz))
            t = p * inv
            values = (r, mx, my, mz, e, s, vx, vy, vz, p, jnp.sqrt(GAMMA * t), t, kap[j])
            for i, value in enumerate(values):
                q[i, z, j] = value

    z_faces(q, zf, 0, 4)
    keep = (row < 6) | (arrival[...] > 0.5)
    final[:, 128:160, :] = jnp.zeros((6, 32, LANES), jnp.float32)

    @pl.loop(1, 5)
    def _(z):
        def emit(f, j, value):
            done = 0.5 * (state[f, z, j] + q[f, z, j]) - (0.25 * step) * value
            final[f, pl.ds(4 * j + z - 1, 8, stride=16), :] = jnp.where(keep, done, 0.0)

        divergence(q, zf, z, 4, emit)

    copy = pltpu.make_async_copy(final.at[:, pl.ds(pl.multiple_of(flags[0] * 32, 32), 128), :], out, sem)
    copy.start()
    copy.wait()


def swap(x, partner):
    m, n = lax.axis_size("curve"), lax.axis_size("near")
    route = []
    for c in range(m):
        for i in range(n):
            to_c, to_i = partner(c, i)
            route.append((c * n + i, to_c * n + to_i))
    return lax.ppermute(x, ("curve", "near"), route)


def largest(x):
    m, n = lax.axis_size("curve"), lax.axis_size("near")
    x = jnp.maximum(x, swap(x, lambda c, i: (c, i ^ 1)))
    x = jnp.maximum(x, swap(x, lambda c, i: (c, ((i + 1) ^ 1) - 1 if 0 < i < n - 1 else n - 1 - i)))
    reach = 4
    while reach < n:
        x = jnp.maximum(x, swap(x, lambda c, i, d=reach: (c, (i + d) % n)))
        reach *= 2
    reach = 1
    while reach < m:
        if m % (2 * reach) == 0:
            x = jnp.maximum(x, swap(x, lambda c, i, d=reach: (c ^ d, i ^ 1)))
        else:
            x = jnp.maximum(x, swap(x, lambda c, i, d=reach: ((c + d) % m, i ^ 1)))
        reach *= 2
    return x


def rows_view(x):
    lead, cells = x.shape[:-2], x.shape[-1]
    x = x.reshape(lead + (4, cells // LANES, LANES))
    return jnp.swapaxes(x, -3, -2).reshape(lead + (4 * (cells // LANES), LANES))


def local(primitive, conductivity, new_owner):
    segment = lax.axis_index("curve")
    m = lax.axis_size("curve")
    rows = primitive.shape[2] // LANES * 4
    half = rows // 2
    prim, kappa = rows_view(primitive), rows_view(conductivity)
    flags = (new_owner[0:1] != segment).astype(jnp.int32)

    to_before, to_after, msg_a, msg_b, peak = pl.pallas_call(
        pack_kernel,
        out_shape=(f32(7, 40, LANES), f32(7, 4, LANES), f32(7, half, LANES), f32(7, half, LANES), f32(2, LANES)),
        in_specs=[VMEM, VMEM, SMEM],
        out_specs=(VMEM,) * 5,
        compiler_params=PARAMS,
        name="pack",
    )(prim, kappa, flags)

    right = lax.ppermute(to_before, "curve", [(c, (c - 1) % m) for c in range(m)])
    left = lax.ppermute(to_after, "curve", [(c, (c + 1) % m) for c in range(m)])
    n = lax.axis_size("near")
    with_a = lambda c, i: (c, i ^ 1)
    with_b = lambda c, i: (c, ((i + 1) ^ 1) - 1 if 0 < i < n - 1 else n - 1 - i)
    rec_a, rec_b = swap(msg_a, with_a), swap(msg_b, with_b)
    cor_a, cor_b = pl.pallas_call(
        corner_kernel,
        out_shape=(f32(7, 32, LANES), f32(7, 32, LANES)),
        in_specs=[VMEM, VMEM],
        out_specs=(VMEM, VMEM),
        compiler_params=PARAMS,
        name="corners",
    )(right, left)
    cor_a, cor_b = swap(cor_a, with_a), swap(cor_b, with_b)
    peak = largest(peak)

    state, total, conduct, arrival = pl.pallas_call(
        first_kernel,
        out_shape=(f32(6, 6, 5, 8, LANES), f32(6, 6, 5, 8, LANES), f32(6, 5, 8, LANES), f32(8, LANES)),
        in_specs=[VMEM] * 8,
        out_specs=(VMEM,) * 4,
        scratch_shapes=[
            pltpu.VMEM((7, 8, 40, LANES), jnp.float32),
            pltpu.VMEM((NQ, 8, 5, 8, LANES), jnp.float32),
            pltpu.VMEM((6, 5, 8, LANES), jnp.float32),
        ],
        compiler_params=PARAMS,
        name="first_section",
    )(prim, kappa, right, left, rec_a, rec_b, cor_a, cor_b)

    out = pl.pallas_call(
        second_kernel,
        out_shape=f32(6, rows + 32, LANES),
        in_specs=[VMEM] * 5 + [SMEM],
        out_specs=pl.BlockSpec(memory_space=pl.ANY),
        scratch_shapes=[
            pltpu.VMEM((NQ, 6, 5, 8, LANES), jnp.float32),
            pltpu.VMEM((6, 5, 8, LANES), jnp.float32),
            pltpu.VMEM((6, rows + 64, LANES), jnp.float32),
            pltpu.SemaphoreType.DMA,
        ],
        compiler_params=PARAMS,
        name="second_section",
    )(state, total, conduct, arrival, peak, flags)
    out = jnp.swapaxes(out.reshape(6, (rows + 32) // 4, 4, LANES), 1, 2)
    return out.reshape(1, 6, 4, (rows + 32) // 4 * LANES)


def solution(mesh):
    in_specs = (P(None, "near", "curve"), P("near", "curve"), P("curve"))
    out_specs = P("curve", None, "near", None)
    return jax.shard_map(local, mesh=mesh, in_specs=in_specs, out_specs=out_specs, check_vma=False)
```

```python
import functools

import jax
import jax.numpy as jnp
from jax import lax
from jax.experimental import pallas as pl
from jax.experimental.pallas import tpu as pltpu
from jax.sharding import PartitionSpec as P

BW = 32
LANES = 128
PLANES = LANES // BW
GAMMA = 1.4
COURANT = 0.8
NQ = 13
VX, PR, SND, TMP, KAP = 6, 9, 10, 11, 12
VMEM = pl.BlockSpec(memory_space=pltpu.VMEM)
SMEM = pl.BlockSpec(memory_space=pltpu.SMEM)
PARAMS = pltpu.CompilerParams(vmem_limit_bytes=24 * 1024 * 1024)


def f32(*shape):
    return jax.ShapeDtypeStruct(shape, jnp.float32)


def lanes_of(shape):
    return lax.broadcasted_iota(jnp.int32, shape, 1)


def rows_of(shape):
    return lax.broadcasted_iota(jnp.int32, shape, 0)


def pack_kernel(prim, kappa, flags, to_before, to_after, msg_a, msg_b, peak):
    even = lax.axis_index("near") % 2 == 0
    blocks = prim.shape[1] // 4

    def source(f):
        return (prim, (f,)) if f < 6 else (kappa, ())

    for f in range(7):
        ref, at = source(f)
        to_before[f, 0:36, :] = ref[at + (pl.ds(0, 36), slice(None))]
        to_after[f] = ref[at + (pl.ds(4 * blocks - 4, 4), slice(None))]
        for msg, start in ((msg_a, jnp.where(even, 2, 0)), (msg_b, jnp.where(even, 0, 2))):
            for z in range(2):
                for g in range(blocks // 8):
                    msg[f, z * blocks + 8 * g : z * blocks + 8 * g + 8, :] = ref[
                        at + (pl.ds(start + z + 32 * g, 8, stride=4), slice(None))
                    ]
    leaving = flags[0].astype(jnp.float32)
    to_before[:, 36:40, :] = jnp.full((7, 4, LANES), leaving, jnp.float32)
    speed = top = None
    for g in range(prim.shape[1] // 8):
        rows = pl.ds(8 * g, 8)
        sound = jnp.sqrt(GAMMA * prim[4, rows, :] / prim[0, rows, :])
        s = jnp.abs(prim[1, rows, :]) + jnp.abs(prim[2, rows, :]) + jnp.abs(prim[3, rows, :]) + 3.0 * sound
        k = kappa[rows, :]
        speed = s if speed is None else jnp.maximum(speed, s)
        top = k if top is None else jnp.maximum(top, k)
    peak[0:1, :] = jnp.max(speed, axis=0, keepdims=True)
    peak[1:2, :] = jnp.max(top, axis=0, keepdims=True)


def corner_kernel(right, left, corner_a, corner_b):
    even = lax.axis_index("near") % 2 == 0
    for msg, start in ((corner_a, jnp.where(even, 2, 0)), (corner_b, jnp.where(even, 0, 2))):
        for f in range(7):
            for z in range(2):
                msg[f, 16 * z : 16 * z + 8, :] = right[f, pl.ds(start + z, 8, stride=4), :]
                msg[f, pl.ds(16 * z + 8, 1), :] = right[f, pl.ds(32 + start + z, 1), :]
                msg[f, pl.ds(16 * z + 9, 1), :] = left[f, pl.ds(start + z, 1), :]


def up_x(q, lane):
    w = [pltpu.roll(v, LANES - BW, 1) for v in q[:4]]
    w.append(pltpu.roll(w[0], 7, 0))
    return [jnp.where(lane < LANES - BW, w[j], w[j + 1]) for j in range(4)] + [pltpu.roll(q[4], LANES - BW, 1)]


def up_y(v, low):
    return jnp.where(low == BW - 1, pltpu.roll(v, BW - 1, 1), pltpu.roll(v, LANES - 1, 1))


def down_y(v, low):
    return jnp.where(low == 0, pltpu.roll(v, LANES - BW + 1, 1), pltpu.roll(v, 1, 1))


def face(lower_u, upper_u, lower_f, upper_f, speed, heat):
    out = (lower_f + upper_f) - speed * (upper_u - lower_u)
    return out if heat is None else out - heat


def z_face_row(q, z, slots):
    speed, heat = [], []
    for j in range(slots):
        s0 = jnp.abs(q[VX + 2, z, j]) + q[SND, z, j]
        s1 = jnp.abs(q[VX + 2, z + 1, j]) + q[SND, z + 1, j]
        speed.append(jnp.maximum(s0, s1))
        heat.append((q[KAP, z, j] + q[KAP, z + 1, j]) * (q[TMP, z + 1, j] - q[TMP, z, j]))
    return {
        (f, j): face(
            q[f, z, j],
            q[f, z + 1, j],
            physical(q, f, j, 2, z),
            physical(q, f, j, 2, z + 1),
            speed[j],
            heat[j] if f == 4 else None,
        )
        for f in range(6)
        for j in range(slots)
    }


def physical(q, f, j, k, z):
    if f == 0:
        return q[1 + k, z, j]
    v = q[VX + k, z, j]
    if f == 4:
        return (q[4, z, j] + q[PR, z, j]) * v
    out = q[f, z, j] * v
    return out + q[PR, z, j] if f == 1 + k else out


def z_faces(q, zf, z, slots):
    for key, value in z_face_row(q, z, slots).items():
        zf[key] = value


def divergence(q, zf, z, slots, emit):
    shape = (8, LANES)
    lane, row = lanes_of(shape), rows_of(shape)
    low = lane & (BW - 1)
    ghost = 4
    five = range(5)
    at = lambda i, j: q[i, z, j]
    sx = [jnp.abs(at(VX, j)) + at(SND, j) for j in five]
    sy = [jnp.abs(at(VX + 1, j)) + at(SND, j) for j in range(slots)]
    kx, tx = [at(KAP, j) for j in five], [at(TMP, j) for j in five]
    sxu, kxu, txu = up_x(sx, lane), up_x(kx, lane), up_x(tx, lane)
    syu, kyu, tyu = ([up_y(v, low) for v in vs[:slots]] for vs in (sy, kx, tx))
    ax = [jnp.maximum(v, w) for v, w in zip(sx, sxu, strict=True)]
    ay = [jnp.maximum(v, w) for v, w in zip(sy, syu, strict=True)]
    hx = [(kx[j] + kxu[j]) * (txu[j] - tx[j]) for j in five]
    hy = [(kx[j] + kyu[j]) * (tyu[j] - tx[j]) for j in range(slots)]

    def neighbours(f):
        u = [at(f, j) for j in five]
        fx = [physical(q, f, j, 0, z) for j in five]
        fy = [physical(q, f, j, 1, z) for j in range(slots)]
        return u, fx, fy, up_x(u, lane), up_x(fx, lane), [up_y(v, low) for v in u[:slots]], [up_y(v, low) for v in fy]

    def sides(f, u, fx, fy, ux, fux, uy, fuy):
        heat = lambda h: h if f == 4 else None
        gx = [face(u[j], ux[j], fx[j], fux[j], ax[j], heat(hx[j])) for j in five]
        gx[3] = jnp.where((lane >= LANES - BW) & (row == 7), gx[ghost], gx[3])
        d = [pltpu.roll(g, BW, 1) for g in gx]
        before = jnp.where(row == 0, d[ghost], pltpu.roll(d[3], 1, 0))
        dx = [jnp.where(lane >= BW, d[j], before if j == 0 else d[j - 1]) for j in range(4)] + [d[ghost]]
        gy = [face(u[j], uy[j], fy[j], fuy[j], ay[j], heat(hy[j])) for j in range(slots)]
        dy = [down_y(g, low) for g in gy]
        return [(gx[j] - dx[j]) + (gy[j] - dy[j]) for j in range(slots)]

    near = [neighbours(f) for f in range(6)]
    gz = z_face_row(q, z, slots)
    part = [sides(f, *near[f]) for f in range(6)]
    total = {key: part[key[0]][key[1]] + (value - zf[key]) for key, value in gz.items()}
    emit(total)
    for key, value in gz.items():
        zf[key] = value


def first_kernel(
    prim, kappa, right, left, rec_a, rec_b, cor_a, cor_b, q, total, arrival, ext, zf
):
    segment, segments = lax.axis_index("curve"), lax.axis_size("curve")
    even = lax.axis_index("near") % 2 == 0
    blocks = prim.shape[1] // 4
    shape = (8, LANES)
    lane, row = lanes_of(shape), rows_of(shape)
    first, last = segment == 0, segment == segments - 1
    base_a, base_b = jnp.where(even, 6, 0), jnp.where(even, 0, 6)
    spread = lambda x: jnp.broadcast_to(x, shape)

    arrival[...] = jnp.where(last, 0.0, spread(right[0, 36:37, :]))

    def filled(own, box, beyond, behind):
        edge = spread(own[-1][7:8])
        box = jnp.where(last, pltpu.roll(edge, BW, 1), box)
        start, end = spread(own[0][0:1]), spread(box[7:8])
        behind = jnp.where(first, pltpu.roll(start, LANES - BW, 1), spread(behind))
        low_side = jnp.where(lane < BW, start, behind)
        high_side = jnp.where(lane >= LANES - BW, end, spread(beyond))
        return own + [box, jnp.where(row == 7, high_side, low_side)]

    for f in range(7):
        ref, at = (prim, (f,)) if f < 6 else (kappa, ())
        parts = []
        for z in range(4):
            own = [ref[at + (pl.ds(z + 32 * g, 8, stride=4), slice(None))] for g in range(blocks // 8)]
            rows = filled(own, right[f, pl.ds(z, 8, stride=4), :], right[f, 32 + z : 33 + z, :], left[f, z : z + 1, :])
            parts.append((z + 2, rows))
        for rec, cor, base in ((rec_a, cor_a, base_a), (rec_b, cor_b, base_b)):
            for z in range(2):
                own = [rec[f, z * blocks + 8 * g : z * blocks + 8 * g + 8, :] for g in range(blocks // 8)]
                c = 16 * z
                rows = filled(own, cor[f, c : c + 8, :], cor[f, c + 8 : c + 9, :], cor[f, c + 9 : c + 10, :])
                parts.append((base + z, rows))
        for z, rows in parts:
            for g, value in enumerate(rows):
                ext[f, z, 8 * g : 8 * g + 8, :] = value

    @pl.loop(0, 8)
    def _(z):
        found = []
        for j in range(5):
            rows = pl.ds(j, 8, stride=4) if j < 4 else pl.ds(32, 8)
            r, vx, vy, vz, p, s, k = (ext[f, z, rows, :] for f in range(7))
            t = p / r
            u = (r, r * vx, r * vy, r * vz, p / (GAMMA - 1.0) + 0.5 * r * (vx * vx + vy * vy + vz * vz), r * s)
            found.append(u + (vx, vy, vz, p, jnp.sqrt(GAMMA * t), t, k))
        for j, values in enumerate(found):
            for i, value in enumerate(values):
                q[i, z, j] = value

    z_faces(q, zf, 0, 5)

    @pl.loop(1, 7)
    def _(z):
        def emit(values):
            for (f, j), value in values.items():
                total[f, z - 1, j] = value

        divergence(q, zf, z, 5, emit)


def second_kernel(base, total, arrival, peak, flags, out, q, zf, final, sem):
    segment, segments = lax.axis_index("curve"), lax.axis_size("curve")
    shape = (8, LANES)
    lane, row = lanes_of(shape), rows_of(shape)
    first, last = segment == 0, segment == segments - 1
    speed, top = jnp.max(peak[0:1, :]), jnp.max(peak[1:2, :])
    step = COURANT / (speed + 6.0 * top)
    own_boxes = 3 * LANES

    @pl.loop(0, 6)
    def _(z):
        half = [[base[f, z + 1, j] - (0.5 * step) * total[f, z, j] for j in range(5)] for f in range(6)]
        kap = [base[KAP, z + 1, j] for j in range(5)]
        for u in half + [kap]:
            edge = pltpu.roll(pltpu.roll(u[3], BW, 1), 1, 0)
            u[0] = jnp.where(last & (row == 6) & (lane < BW), edge, u[0])
            g = jnp.where((row == 0) & (lane < BW), u[0], u[4])
            g = jnp.where((row == 7) & (lane >= LANES - BW), u[3], g)
            u[4] = jnp.where(first & (row == 0) & (lane >= BW), pltpu.roll(g, LANES - BW, 1), g)
        found = []
        for j in range(5):
            r, mx, my, mz, e, s = (half[f][j] for f in range(6))
            inv = 1.0 / r
            vx, vy, vz = mx * inv, my * inv, mz * inv
            p = (GAMMA - 1.0) * (e - 0.5 * (mx * vx + my * vy + mz * vz))
            t = p * inv
            found.append((r, mx, my, mz, e, s, vx, vy, vz, p, jnp.sqrt(GAMMA * t), t, kap[j]))
        for j, values in enumerate(found):
            for i, value in enumerate(values):
                q[i, z, j] = value

    z_faces(q, zf, 0, 4)
    keep = (row < 6) | (arrival[...] > 0.5)
    final[:, 128:160, :] = jnp.zeros((6, 32, LANES), jnp.float32)

    @pl.loop(1, 5)
    def _(z):
        def emit(values):
            done = {
                (f, j): 0.5 * (base[f, z + 1, j] + q[f, z, j]) - (0.25 * step) * value
                for (f, j), value in values.items()
            }
            for (f, j), value in done.items():
                final[f, pl.ds(4 * j + z - 1, 8, stride=16), :] = jnp.where(keep, value, 0.0)

        divergence(q, zf, z, 4, emit)

    copy = pltpu.make_async_copy(final.at[:, pl.ds(pl.multiple_of(flags[0] * 32, 32), 128), :], out, sem)
    copy.start()
    copy.wait()


def swap(x, partner):
    m, n = lax.axis_size("curve"), lax.axis_size("near")
    route = []
    for c in range(m):
        for i in range(n):
            to_c, to_i = partner(c, i)
            route.append((c * n + i, to_c * n + to_i))
    return lax.ppermute(x, ("curve", "near"), route)


def largest(x):
    m, n = lax.axis_size("curve"), lax.axis_size("near")
    x = jnp.maximum(x, swap(x, lambda c, i: (c, i ^ 1)))
    x = jnp.maximum(x, swap(x, lambda c, i: (c, ((i + 1) ^ 1) - 1 if 0 < i < n - 1 else n - 1 - i)))
    reach = 4
    while reach < n:
        x = jnp.maximum(x, swap(x, lambda c, i, d=reach: (c, (i + d) % n)))
        reach *= 2
    reach = 1
    while reach < m:
        if m % (2 * reach) == 0:
            x = jnp.maximum(x, swap(x, lambda c, i, d=reach: (c ^ d, i ^ 1)))
        else:
            x = jnp.maximum(x, swap(x, lambda c, i, d=reach: ((c + d) % m, i ^ 1)))
        reach *= 2
    return x


def rows_view(x):
    lead, cells = x.shape[:-2], x.shape[-1]
    x = x.reshape(lead + (4, cells // LANES, LANES))
    return jnp.swapaxes(x, -3, -2).reshape(lead + (4 * (cells // LANES), LANES))


def local(primitive, conductivity, new_owner):
    segment = lax.axis_index("curve")
    m = lax.axis_size("curve")
    rows = primitive.shape[2] // LANES * 4
    half = rows // 2
    prim, kappa = rows_view(primitive), rows_view(conductivity)
    flags = (new_owner[0:1] != segment).astype(jnp.int32)

    to_before, to_after, msg_a, msg_b, peak = pl.pallas_call(
        pack_kernel,
        out_shape=(f32(7, 40, LANES), f32(7, 4, LANES), f32(7, half, LANES), f32(7, half, LANES), f32(2, LANES)),
        in_specs=[VMEM, VMEM, SMEM],
        out_specs=(VMEM,) * 5,
        compiler_params=PARAMS,
        name="pack",
    )(prim, kappa, flags)

    right = lax.ppermute(to_before, "curve", [(c, (c - 1) % m) for c in range(m)])
    left = lax.ppermute(to_after, "curve", [(c, (c + 1) % m) for c in range(m)])
    n = lax.axis_size("near")
    with_a = lambda c, i: (c, i ^ 1)
    with_b = lambda c, i: (c, ((i + 1) ^ 1) - 1 if 0 < i < n - 1 else n - 1 - i)
    rec_a, rec_b = swap(msg_a, with_a), swap(msg_b, with_b)
    cor_a, cor_b = pl.pallas_call(
        corner_kernel,
        out_shape=(f32(7, 32, LANES), f32(7, 32, LANES)),
        in_specs=[VMEM, VMEM],
        out_specs=(VMEM, VMEM),
        compiler_params=PARAMS,
        name="corners",
    )(right, left)
    cor_a, cor_b = swap(cor_a, with_a), swap(cor_b, with_b)
    peak = largest(peak)

    base, total, arrival = pl.pallas_call(
        first_kernel,
        out_shape=(f32(NQ, 8, 5, 8, LANES), f32(6, 6, 5, 8, LANES), f32(8, LANES)),
        in_specs=[VMEM] * 8,
        out_specs=(VMEM,) * 3,
        scratch_shapes=[
            pltpu.VMEM((7, 8, 40, LANES), jnp.float32),
            pltpu.VMEM((6, 5, 8, LANES), jnp.float32),
        ],
        compiler_params=PARAMS,
        name="first_section",
    )(prim, kappa, right, left, rec_a, rec_b, cor_a, cor_b)

    out = pl.pallas_call(
        second_kernel,
        out_shape=f32(6, rows + 32, LANES),
        in_specs=[VMEM] * 4 + [SMEM],
        out_specs=pl.BlockSpec(memory_space=pl.ANY),
        scratch_shapes=[
            pltpu.VMEM((NQ, 6, 5, 8, LANES), jnp.float32),
            pltpu.VMEM((6, 5, 8, LANES), jnp.float32),
            pltpu.VMEM((6, rows + 64, LANES), jnp.float32),
            pltpu.SemaphoreType.DMA,
        ],
        compiler_params=PARAMS,
        name="second_section",
    )(base, total, arrival, peak, flags)
    out = jnp.swapaxes(out.reshape(6, (rows + 32) // 4, 4, LANES), 1, 2)
    return out.reshape(1, 6, 4, (rows + 32) // 4 * LANES)


def solution(mesh):
    in_specs = (P(None, "near", "curve"), P("near", "curve"), P("curve"))
    out_specs = P("curve", None, "near", None)
    return jax.shard_map(local, mesh=mesh, in_specs=in_specs, out_specs=out_specs, check_vma=False)
```

```python
import functools

import jax
import jax.numpy as jnp
from jax import lax
from jax.experimental import pallas as pl
from jax.experimental.pallas import tpu as pltpu
from jax.sharding import PartitionSpec as P

BW = 32
LANES = 128
PLANES = LANES // BW
GAMMA = 1.4
COURANT = 0.8
DEP_C, DEP_D, DEP_S, DEP_I, COST_I = 0, 1, 3, 4, 2
NQ = 13
VX, PR, SND, TMP, KAP = 6, 9, 10, 11, 12
VMEM = pl.BlockSpec(memory_space=pltpu.VMEM)
PARAMS = pltpu.CompilerParams(vmem_limit_bytes=24 * 1024 * 1024)


def f32(*shape):
    return jax.ShapeDtypeStruct(shape, jnp.float32)


def lanes_of(shape):
    return lax.broadcasted_iota(jnp.int32, shape, 1)


def rows_of(shape):
    return lax.broadcasted_iota(jnp.int32, shape, 0)


def load_kernel(prim, kappa, new_owner, own, peak, leaving, owner, sems):
    total = own.shape[1]
    copies = [
        pltpu.make_async_copy(prim, own.at[pl.ds(0, 6)], sems.at[0]),
        pltpu.make_async_copy(kappa, own.at[6], sems.at[1]),
        pltpu.make_async_copy(new_owner, owner, sems.at[2]),
    ]
    for copy in copies:
        copy.start()
    for copy in copies:
        copy.wait()
    speed = top = None
    for g in range(total // 8):
        r = pl.ds(8 * g, 8)
        sound = jnp.sqrt(GAMMA * own[4, r, :] / own[0, r, :])
        s = jnp.abs(own[1, r, :]) + jnp.abs(own[2, r, :]) + jnp.abs(own[3, r, :]) + 3.0 * sound
        speed = s if speed is None else jnp.maximum(speed, s)
        top = own[6, r, :] if top is None else jnp.maximum(top, own[6, r, :])
    peak[0:1, :] = jnp.max(speed, axis=0, keepdims=True)
    peak[1:2, :] = jnp.max(top, axis=0, keepdims=True)
    leaves = (owner[0] != lax.axis_index("curve")).astype(jnp.float32)
    leaving[...] = jnp.full(leaving.shape, leaves, jnp.float32)


def side_kernel(upper_when_even, own, leaving, order, msg):
    even = lax.axis_index("curve") % 2 == 0
    box = jnp.logical_not(even) if upper_when_even else even
    total = own.shape[1]
    for g in range(5):
        length = 8 if g < 4 else 4
        first, last = pl.ds(8 * g, length), pl.ds(total - 36 + 8 * g, length)
        parts = [jnp.where(box, own[f, first, :], own[f, last, :]) for f in range(7)]
        for f in range(7):
            msg[f, first, :] = parts[f]
    for f in range(7):
        msg[f, 36:40, :] = leaving[0:4, :]


def spread_kernel(own, rec_c, rec_d, peak, ext, msg_a, msg_b, arrival, peak_out):
    segment, segments = lax.axis_index("curve"), lax.axis_size("curve")
    first, last = segment == 0, segment == segments - 1
    odd = segment % 2 == 1
    even_slab = lax.axis_index("near") % 2 == 0
    groups = own.shape[1] // 32
    shape = (8, LANES)
    lane, row = lanes_of(shape), rows_of(shape)
    spread = lambda x: jnp.broadcast_to(x, shape)
    peak_out[...] = peak[...]
    arrival[...] = jnp.where(last, 0.0, spread(jnp.where(odd, rec_d[0, 36:37, :], rec_c[0, 36:37, :])))
    for f in range(7):
        out = []
        for z in range(4):
            cells = [own[f, pl.ds(z + 32 * g, 8, stride=4), :] for g in range(groups)]
            at = pl.ds(z, 8, stride=4)
            box = jnp.where(odd, rec_d[f, at, :], rec_c[f, at, :])
            beyond = spread(jnp.where(odd, rec_d[f, 32 + z : 33 + z, :], rec_c[f, 32 + z : 33 + z, :]))
            behind = spread(jnp.where(odd, rec_c[f, 32 + z : 33 + z, :], rec_d[f, 32 + z : 33 + z, :]))
            edge = pltpu.roll(spread(cells[-1][7:8]), BW, 1)
            box = jnp.where(last, edge, box)
            start, end = spread(cells[0][0:1]), spread(box[7:8])
            behind = jnp.where(first, pltpu.roll(start, LANES - BW, 1), behind)
            low_side = jnp.where(lane < BW, start, behind)
            high_side = jnp.where(lane >= LANES - BW, end, beyond)
            out.append(cells + [box, jnp.where(row == 7, high_side, low_side)])
        for z in range(4):
            for g, value in enumerate(out[z]):
                ext[f, z, 8 * g : 8 * g + 8, :] = value
        for msg, up in ((msg_a, even_slab), (msg_b, jnp.logical_not(even_slab))):
            for z in range(2):
                for g in range(groups + 2):
                    value = jnp.where(up, out[z + 2][g], out[z][g])
                    if g < groups + 1:
                        msg[f, 36 * z + 8 * g : 36 * z + 8 * g + 8, :] = value
                    else:
                        msg[f, 36 * z + 32 : 36 * z + 33, :] = value[0:1]
                        msg[f, 36 * z + 33 : 36 * z + 34, :] = value[7:8]


def up_x(q, lane):
    w = [pltpu.roll(v, LANES - BW, 1) for v in q[:4]]
    w.append(pltpu.roll(w[0], 7, 0))
    return [jnp.where(lane < LANES - BW, w[j], w[j + 1]) for j in range(4)] + [pltpu.roll(q[4], LANES - BW, 1)]


def up_y(v, low):
    return jnp.where(low == BW - 1, pltpu.roll(v, BW - 1, 1), pltpu.roll(v, LANES - 1, 1))


def down_y(v, low):
    return jnp.where(low == 0, pltpu.roll(v, LANES - BW + 1, 1), pltpu.roll(v, 1, 1))


def face(lower_u, upper_u, lower_f, upper_f, speed, heat):
    out = (lower_f + upper_f) - speed * (upper_u - lower_u)
    return out if heat is None else out - heat


def z_face_row(q, z, slots):
    speed, heat = [], []
    for j in range(slots):
        s0 = jnp.abs(q[VX + 2, z, j]) + q[SND, z, j]
        s1 = jnp.abs(q[VX + 2, z + 1, j]) + q[SND, z + 1, j]
        speed.append(jnp.maximum(s0, s1))
        heat.append((q[KAP, z, j] + q[KAP, z + 1, j]) * (q[TMP, z + 1, j] - q[TMP, z, j]))
    return {
        (f, j): face(
            q[f, z, j],
            q[f, z + 1, j],
            physical(q, f, j, 2, z),
            physical(q, f, j, 2, z + 1),
            speed[j],
            heat[j] if f == 4 else None,
        )
        for f in range(6)
        for j in range(slots)
    }


def physical(q, f, j, k, z):
    if f == 0:
        return q[1 + k, z, j]
    v = q[VX + k, z, j]
    if f == 4:
        return (q[4, z, j] + q[PR, z, j]) * v
    out = q[f, z, j] * v
    return out + q[PR, z, j] if f == 1 + k else out


def plane_divergence(q, z, slots):
    shape = (8, LANES)
    lane, row = lanes_of(shape), rows_of(shape)
    low = lane & (BW - 1)
    ghost = 4
    five = range(5)
    at = lambda i, j: q[i, z, j]
    sx = [jnp.abs(at(VX, j)) + at(SND, j) for j in five]
    sy = [jnp.abs(at(VX + 1, j)) + at(SND, j) for j in range(slots)]
    kx, tx = [at(KAP, j) for j in five], [at(TMP, j) for j in five]
    sxu, kxu, txu = up_x(sx, lane), up_x(kx, lane), up_x(tx, lane)
    syu, kyu, tyu = ([up_y(v, low) for v in vs[:slots]] for vs in (sy, kx, tx))
    ax = [jnp.maximum(v, w) for v, w in zip(sx, sxu, strict=True)]
    ay = [jnp.maximum(v, w) for v, w in zip(sy, syu, strict=True)]
    hx = [(kx[j] + kxu[j]) * (txu[j] - tx[j]) for j in five]
    hy = [(kx[j] + kyu[j]) * (tyu[j] - tx[j]) for j in range(slots)]

    def neighbours(f):
        u = [at(f, j) for j in five]
        fx = [physical(q, f, j, 0, z) for j in five]
        fy = [physical(q, f, j, 1, z) for j in range(slots)]
        return u, fx, fy, up_x(u, lane), up_x(fx, lane), [up_y(v, low) for v in u[:slots]], [up_y(v, low) for v in fy]

    def sides(f, u, fx, fy, ux, fux, uy, fuy):
        heat = lambda h: h if f == 4 else None
        gx = [face(u[j], ux[j], fx[j], fux[j], ax[j], heat(hx[j])) for j in five]
        gx[3] = jnp.where((lane >= LANES - BW) & (row == 7), gx[ghost], gx[3])
        d = [pltpu.roll(g, BW, 1) for g in gx]
        before = jnp.where(row == 0, d[ghost], pltpu.roll(d[3], 1, 0))
        dx = [jnp.where(lane >= BW, d[j], before if j == 0 else d[j - 1]) for j in range(4)] + [d[ghost]]
        gy = [face(u[j], uy[j], fy[j], fuy[j], ay[j], heat(hy[j])) for j in range(slots)]
        dy = [down_y(g, low) for g in gy]
        return [(gx[j] - dx[j]) + (gy[j] - dy[j]) for j in range(slots)]

    near = [neighbours(f) for f in range(6)]
    part = [sides(f, *near[f]) for f in range(6)]
    return {(f, j): part[f][j] for f in range(6) for j in range(slots)}


def raw_quantities(r, vx, vy, vz, p, s, k):
    t = p / r
    energy = p / (GAMMA - 1.0) + 0.5 * r * (vx * vx + vy * vy + vz * vz)
    return (r, r * vx, r * vy, r * vz, energy, r * s, vx, vy, vz, p, jnp.sqrt(GAMMA * t), t, k)


def store_all(ref, at, values):
    for j, quantities in enumerate(values):
        for i, value in enumerate(quantities):
            ref[(i,) + at + (j,)] = value


def inner_kernel(ext, order, q, total):
    @pl.loop(0, 4)
    def _(z):
        found = []
        for j in range(5):
            rows = pl.ds(j, 8, stride=4) if j < 4 else pl.ds(32, 8)
            found.append(raw_quantities(*(ext[f, z, rows, :] for f in range(7))))
        store_all(q, (z,), found)

    @pl.loop(0, 4)
    def _(z):
        values = plane_divergence(q, z, 5)
        for (f, j), value in values.items():
            total[f, z, j] = value

    @pl.loop(0, 3)
    def _(z):
        faces = z_face_row(q, z, 5)
        lower = {(f, j): total[f, z, j] + value for (f, j), value in faces.items()}
        upper = {(f, j): total[f, z + 1, j] - value for (f, j), value in faces.items()}
        for (f, j), value in lower.items():
            total[f, z, j] = value
        for (f, j), value in upper.items():
            total[f, z + 1, j] = value


def outer_kernel(q, inner, rec_a, rec_b, total, edge_q, edge_total, rim):
    even = lax.axis_index("near") % 2 == 0
    shape = (8, LANES)
    row = rows_of(shape)
    spread = lambda x: jnp.broadcast_to(x, shape)

    @pl.loop(0, 4)
    def _(z):
        for f in range(6):
            for j in range(5):
                total[f, z, j] = inner[f, z, j]

    for i in range(NQ):
        for j in range(5):
            rim[i, 2, j] = q[i, 0, j]
            rim[i, 3, j] = q[i, 3, j]
    for rec, base in ((rec_a, jnp.where(even, 4, 0)), (rec_b, jnp.where(even, 0, 4))):

        @pl.loop(0, 2)
        def _(z):
            found = []
            for j in range(5):
                if j < 4:
                    cells = (rec[f, pl.ds(36 * z + j, 8, stride=4), :] for f in range(7))
                else:
                    cells = (
                        jnp.where(row == 7, spread(rec[f, pl.ds(36 * z + 33, 1), :]), spread(rec[f, pl.ds(36 * z + 32, 1), :]))
                        for f in range(7)
                    )
                found.append(raw_quantities(*cells))
            store_all(rim, (base + z,), found)

    @pl.loop(0, 2)
    def _(e):
        z = 1 + 3 * e
        values = plane_divergence(rim, z, 5)
        for (f, j), value in values.items():
            edge_total[f, e, j] = value
        for j in range(5):
            for i, k in enumerate((0, 1, 2, 3, 4, 5, KAP)):
                edge_q[i, e, j] = rim[k, z, j]

    @pl.loop(0, 2)
    def _(e):
        below = z_face_row(rim, 3 * e, 5)
        above = z_face_row(rim, 3 * e + 1, 5)
        own = 3 * e
        change = {key: jnp.where(e == 0, -above[key], below[key]) for key in above}
        edge = {(f, j): edge_total[f, e, j] + (above[f, j] - below[f, j]) for f, j in above}
        done = {(f, j): inner[f, own, j] + value for (f, j), value in change.items()}
        for (f, j), value in edge.items():
            edge_total[f, e, j] = value
        for (f, j), value in done.items():
            total[f, own, j] = value


def second_kernel(base, total, edge_q, edge_total, arrival, peak, new_owner, out, q, zf, final, owner, sems):
    segment, segments = lax.axis_index("curve"), lax.axis_size("curve")
    shape = (8, LANES)
    lane, row = lanes_of(shape), rows_of(shape)
    first, last = segment == 0, segment == segments - 1
    fetch = pltpu.make_async_copy(new_owner, owner, sems.at[0])
    fetch.start()
    speed, top = jnp.max(peak[0:1, :]), jnp.max(peak[1:2, :])
    step = COURANT / (speed + 6.0 * top)

    def half_row(state, divergence, kap_at, source, target):
        half = [
            [state[f, source, j] - (0.5 * step) * divergence[f, source, j] for j in range(5)] for f in range(6)
        ]
        kap = [state[kap_at, source, j] for j in range(5)]
        for u in half + [kap]:
            edge = pltpu.roll(pltpu.roll(u[3], BW, 1), 1, 0)
            u[0] = jnp.where(last & (row == 6) & (lane < BW), edge, u[0])
            g = jnp.where((row == 0) & (lane < BW), u[0], u[4])
            g = jnp.where((row == 7) & (lane >= LANES - BW), u[3], g)
            u[4] = jnp.where(first & (row == 0) & (lane >= BW), pltpu.roll(g, LANES - BW, 1), g)
        found = []
        for j in range(5):
            r, mx, my, mz, e, s = (half[f][j] for f in range(6))
            inv = 1.0 / r
            vx, vy, vz = mx * inv, my * inv, mz * inv
            p = (GAMMA - 1.0) * (e - 0.5 * (mx * vx + my * vy + mz * vz))
            t = p * inv
            found.append((r, mx, my, mz, e, s, vx, vy, vz, p, jnp.sqrt(GAMMA * t), t, kap[j]))
        store_all(q, (target,), found)

    @pl.loop(0, 4)
    def _(z):
        half_row(base, total, KAP, z, z + 1)

    @pl.loop(0, 2)
    def _(e):
        half_row(edge_q, edge_total, 6, e, 5 * e)

    for key, value in z_face_row(q, 0, 4).items():
        zf[key] = value
    keep = (row < 6) | (arrival[...] > 0.5)
    final[:, 128:160, :] = jnp.zeros((6, 32, LANES), jnp.float32)

    @pl.loop(1, 5)
    def _(z):
        plane = plane_divergence(q, z, 4)
        faces = z_face_row(q, z, 4)
        done = {}
        for (f, j), value in faces.items():
            change = plane[f, j] + (value - zf[f, j])
            done[f, j] = 0.5 * (base[f, z - 1, j] + q[f, z, j]) - (0.25 * step) * change
        for (f, j), value in done.items():
            final[f, pl.ds(4 * j + z - 1, 8, stride=16), :] = jnp.where(keep, value, 0.0)
        for key, value in faces.items():
            zf[key] = value

    fetch.wait()
    start = jnp.where(owner[0] != segment, 32, 0)
    copy = pltpu.make_async_copy(final.at[:, pl.ds(pl.multiple_of(start, 32), 128), :], out, sems.at[1])
    copy.start()
    copy.wait()


def swap(x, partner):
    m, n = lax.axis_size("curve"), lax.axis_size("near")
    route = []
    for c in range(m):
        for i in range(n):
            to_c, to_i = partner(c, i)
            route.append((c * n + i, to_c * n + to_i))
    return lax.ppermute(x, ("curve", "near"), route)


def near_routes(n):
    routes = [lambda c, i: (c, i ^ 1), lambda c, i: (c, outer_partner(i, n))]
    reach = 4
    while reach < n:
        routes.append(lambda c, i, d=reach: (c, (i + d) % n))
        reach *= 2
    return routes


def curve_routes(m):
    routes, reach = [], 1
    while reach < m:
        if m % (2 * reach) == 0:
            routes.append(lambda c, i, d=reach: (c ^ d, i ^ 1))
        else:
            routes.append(lambda c, i, d=reach: ((c + d) % m, i ^ 1))
        reach *= 2
    return routes


def outer_partner(i, n):
    return ((i + 1) ^ 1) - 1 if 0 < i < n - 1 else n - 1 - i


def rows_view(x):
    lead, cells = x.shape[:-2], x.shape[-1]
    x = x.reshape(lead + (4, cells // LANES, LANES))
    return jnp.swapaxes(x, -3, -2).reshape(lead + (4 * (cells // LANES), LANES))


def kernel(body, name, ins, outs, scratch=(), us=0):
    cost = pl.CostEstimate(flops=int(us * 1e9), bytes_accessed=int(us * 3e6), transcendentals=0) if us else None
    return pl.pallas_call(
        body,
        out_shape=outs,
        in_specs=ins,
        out_specs=jax.tree.map(lambda _: VMEM, outs),
        scratch_shapes=scratch,
        compiler_params=PARAMS,
        cost_estimate=cost,
        name=name,
    )


def local(primitive, conductivity, new_owner):
    m, n = lax.axis_size("curve"), lax.axis_size("near")
    rows = primitive.shape[2] // LANES * 4
    in_hbm = lambda x: pltpu.with_memory_space_constraint(x, pltpu.HBM)
    prim, kappa, new_owner = in_hbm(rows_view(primitive)), in_hbm(rows_view(conductivity)), in_hbm(new_owner)
    hbm = pl.BlockSpec(memory_space=pltpu.HBM)

    own, peak, leaving = kernel(
        load_kernel,
        "load",
        [hbm, hbm, hbm],
        (f32(7, rows, LANES), f32(2, LANES), f32(8, LANES)),
        [pltpu.SMEM(new_owner.shape, jnp.int32), pltpu.SemaphoreType.DMA((3,))],
    )(prim, kappa, new_owner)

    side = lambda upper, name: kernel(functools.partial(side_kernel, upper), name, [VMEM] * 3, f32(7, 40, LANES))
    peaks = [peak]
    for stage, route in enumerate(near_routes(n) + curve_routes(m)):
        if stage == DEP_C:
            rec_c = swap(side(True, "upper")(own, leaving, peaks[-1]), lambda c, i: (c ^ 1, i))
        if stage == DEP_D:
            msg_d = side(False, "lower")(own, leaving, peaks[-1])
            rec_d = swap(msg_d, lambda c, i: (c, i ^ 1) if c in (0, m - 1) else (outer_partner(c, m), i))
        if stage == DEP_S:
            ext, msg_a, msg_b, arrival, peaks[-1] = kernel(
                spread_kernel,
                "spread",
                [VMEM] * 4,
                (f32(7, 4, 40, LANES), f32(7, 72, LANES), f32(7, 72, LANES), f32(8, LANES), f32(2, LANES)),
            )(own, rec_c, rec_d, peaks[-1])
        peaks.append(jnp.maximum(peaks[-1], swap(peaks[-1], route)))
    rec_a = swap(msg_a, lambda c, i: (c, i ^ 1))
    rec_b = swap(msg_b, lambda c, i: (c, outer_partner(i, n)))

    quantities, sums = f32(NQ, 4, 5, 8, LANES), f32(6, 4, 5, 8, LANES)
    q, inner = kernel(inner_kernel, "inner", [VMEM] * 2, (quantities, sums), us=COST_I)(ext, peaks[DEP_I])
    total, edge_q, edge_total = kernel(
        outer_kernel,
        "outer",
        [VMEM] * 4,
        (sums, f32(7, 2, 5, 8, LANES), f32(6, 2, 5, 8, LANES)),
        [pltpu.VMEM((NQ, 6, 5, 8, LANES), jnp.float32)],
    )(q, inner, rec_a, rec_b)

    out = pl.pallas_call(
        second_kernel,
        out_shape=f32(6, rows + 32, LANES),
        in_specs=[VMEM] * 6 + [hbm],
        out_specs=hbm,
        scratch_shapes=[
            pltpu.VMEM((NQ, 6, 5, 8, LANES), jnp.float32),
            pltpu.VMEM((6, 4, 8, LANES), jnp.float32),
            pltpu.VMEM((6, rows + 64, LANES), jnp.float32),
            pltpu.SMEM(new_owner.shape, jnp.int32),
            pltpu.SemaphoreType.DMA((2,)),
        ],
        compiler_params=PARAMS,
        name="second_section",
    )(q, total, edge_q, edge_total, arrival, peaks[-1], new_owner)
    out = jnp.swapaxes(out.reshape(6, (rows + 32) // 4, 4, LANES), 1, 2)
    return out.reshape(1, 6, 4, (rows + 32) // 4 * LANES)


def solution(mesh):
    in_specs = (P(None, "near", "curve"), P("near", "curve"), P("curve"))
    out_specs = P("curve", None, "near", None)
    return jax.shard_map(local, mesh=mesh, in_specs=in_specs, out_specs=out_specs, check_vma=False)
```

```python
import functools

import jax
import jax.numpy as jnp
from jax import lax
from jax.experimental import pallas as pl
from jax.experimental.pallas import tpu as pltpu
from jax.sharding import PartitionSpec as P

BW = 32
LANES = 128
PLANES = LANES // BW
GAMMA = 1.4
COURANT = 0.8
DEP_C, DEP_D, DEP_B, DEP_S, DEP_I = 0, 1, 2, 3, 3
COST = {"slab": 0, "spread": 0, "inner": 2, "outer": 2}
NQ = 13
VX, PR, SND, TMP, KAP = 6, 9, 10, 11, 12
VMEM = pl.BlockSpec(memory_space=pltpu.VMEM)
PARAMS = pltpu.CompilerParams(vmem_limit_bytes=24 * 1024 * 1024)


def f32(*shape):
    return jax.ShapeDtypeStruct(shape, jnp.float32)


def lanes_of(shape):
    return lax.broadcasted_iota(jnp.int32, shape, 1)


def rows_of(shape):
    return lax.broadcasted_iota(jnp.int32, shape, 0)


def load_kernel(prim, kappa, new_owner, own, peak, leaving, owner, sems):
    total = own.shape[1]
    copies = [
        pltpu.make_async_copy(prim, own.at[pl.ds(0, 6)], sems.at[0]),
        pltpu.make_async_copy(kappa, own.at[6], sems.at[1]),
        pltpu.make_async_copy(new_owner, owner, sems.at[2]),
    ]
    for copy in copies:
        copy.start()
    for copy in copies:
        copy.wait()
    speed = top = None
    for g in range(total // 8):
        r = pl.ds(8 * g, 8)
        sound = jnp.sqrt(GAMMA * own[4, r, :] / own[0, r, :])
        s = jnp.abs(own[1, r, :]) + jnp.abs(own[2, r, :]) + jnp.abs(own[3, r, :]) + 3.0 * sound
        speed = s if speed is None else jnp.maximum(speed, s)
        top = own[6, r, :] if top is None else jnp.maximum(top, own[6, r, :])
    peak[0:1, :] = jnp.max(speed, axis=0, keepdims=True)
    peak[1:2, :] = jnp.max(top, axis=0, keepdims=True)
    leaves = (owner[0] != lax.axis_index("curve")).astype(jnp.float32)
    leaving[...] = jnp.full(leaving.shape, leaves, jnp.float32)


def side_kernel(upper_when_even, own, leaving, order, msg):
    even = lax.axis_index("curve") % 2 == 0
    box = jnp.logical_not(even) if upper_when_even else even
    total = own.shape[1]
    for g in range(5):
        length = 8 if g < 4 else 4
        first, last = pl.ds(8 * g, length), pl.ds(total - 36 + 8 * g, length)
        parts = [jnp.where(box, own[f, first, :], own[f, last, :]) for f in range(7)]
        for f in range(7):
            msg[f, first, :] = parts[f]
    for f in range(7):
        msg[f, 36:40, :] = leaving[0:4, :]


def slab_kernel(own, order, msg):
    up = lax.axis_index("near") % 2 == 1
    groups = own.shape[1] // 32
    for f in range(7):
        parts = {}
        for z in range(2):
            for g in range(groups):
                upper, lower = (own[f, pl.ds(k + 32 * g, 8, stride=4), :] for k in (z + 2, z))
                parts[8 * (groups * z + g)] = jnp.where(up, upper, lower)
        for at, value in parts.items():
            msg[f, at : at + 8, :] = value


def spread_kernel(own, rec_c, rec_d, peak, ext, msg_a, msg_b, arrival, peak_out):
    segment, segments = lax.axis_index("curve"), lax.axis_size("curve")
    first, last = segment == 0, segment == segments - 1
    odd = segment % 2 == 1
    up = lax.axis_index("near") % 2 == 0
    groups = own.shape[1] // 32
    shape = (8, LANES)
    lane, row = lanes_of(shape), rows_of(shape)
    spread = lambda x: jnp.broadcast_to(x, shape)
    peak_out[...] = peak[...]
    arrival[...] = jnp.where(last, 0.0, spread(jnp.where(odd, rec_d[0, 36:37, :], rec_c[0, 36:37, :])))
    for f in range(7):
        out = []
        for z in range(4):
            cells = [own[f, pl.ds(z + 32 * g, 8, stride=4), :] for g in range(groups)]
            at = pl.ds(z, 8, stride=4)
            box = jnp.where(odd, rec_d[f, at, :], rec_c[f, at, :])
            beyond = spread(jnp.where(odd, rec_d[f, 32 + z : 33 + z, :], rec_c[f, 32 + z : 33 + z, :]))
            behind = spread(jnp.where(odd, rec_c[f, 32 + z : 33 + z, :], rec_d[f, 32 + z : 33 + z, :]))
            edge = pltpu.roll(spread(cells[-1][7:8]), BW, 1)
            box = jnp.where(last, edge, box)
            start, end = spread(cells[0][0:1]), spread(box[7:8])
            behind = jnp.where(first, pltpu.roll(start, LANES - BW, 1), behind)
            low_side = jnp.where(lane < BW, start, behind)
            high_side = jnp.where(lane >= LANES - BW, end, beyond)
            out.append(cells + [box, jnp.where(row == 7, high_side, low_side)])
        for z in range(4):
            for g, value in enumerate(out[z]):
                ext[f, z, 8 * g : 8 * g + 8, :] = value
        for msg, ahead, pitch, begin in ((msg_a, up, 36, 0), (msg_b, jnp.logical_not(up), 12, groups)):
            for z in range(2):
                for g in range(begin, groups + 2):
                    value = jnp.where(ahead, out[z + 2][g], out[z][g])
                    at = pitch * z + 8 * (g - begin)
                    if g < groups + 1:
                        msg[f, at : at + 8, :] = value
                    else:
                        msg[f, at : at + 1, :] = value[0:1]
                        msg[f, at + 1 : at + 2, :] = value[7:8]


def up_x(q, lane):
    w = [pltpu.roll(v, LANES - BW, 1) for v in q[:4]]
    w.append(pltpu.roll(w[0], 7, 0))
    return [jnp.where(lane < LANES - BW, w[j], w[j + 1]) for j in range(4)] + [pltpu.roll(q[4], LANES - BW, 1)]


def up_y(v, low):
    return jnp.where(low == BW - 1, pltpu.roll(v, BW - 1, 1), pltpu.roll(v, LANES - 1, 1))


def down_y(v, low):
    return jnp.where(low == 0, pltpu.roll(v, LANES - BW + 1, 1), pltpu.roll(v, 1, 1))


def face(lower_u, upper_u, lower_f, upper_f, speed, heat):
    out = (lower_f + upper_f) - speed * (upper_u - lower_u)
    return out if heat is None else out - heat


def z_face_row(q, z, slots):
    speed, heat = [], []
    for j in range(slots):
        s0 = jnp.abs(q[VX + 2, z, j]) + q[SND, z, j]
        s1 = jnp.abs(q[VX + 2, z + 1, j]) + q[SND, z + 1, j]
        speed.append(jnp.maximum(s0, s1))
        heat.append((q[KAP, z, j] + q[KAP, z + 1, j]) * (q[TMP, z + 1, j] - q[TMP, z, j]))
    return {
        (f, j): face(
            q[f, z, j],
            q[f, z + 1, j],
            physical(q, f, j, 2, z),
            physical(q, f, j, 2, z + 1),
            speed[j],
            heat[j] if f == 4 else None,
        )
        for f in range(6)
        for j in range(slots)
    }


def physical(q, f, j, k, z):
    if f == 0:
        return q[1 + k, z, j]
    v = q[VX + k, z, j]
    if f == 4:
        return (q[4, z, j] + q[PR, z, j]) * v
    out = q[f, z, j] * v
    return out + q[PR, z, j] if f == 1 + k else out


def plane_divergence(q, z, slots):
    shape = (8, LANES)
    lane, row = lanes_of(shape), rows_of(shape)
    low = lane & (BW - 1)
    ghost = 4
    five = range(5)
    at = lambda i, j: q[i, z, j]
    sx = [jnp.abs(at(VX, j)) + at(SND, j) for j in five]
    sy = [jnp.abs(at(VX + 1, j)) + at(SND, j) for j in range(slots)]
    kx, tx = [at(KAP, j) for j in five], [at(TMP, j) for j in five]
    sxu, kxu, txu = up_x(sx, lane), up_x(kx, lane), up_x(tx, lane)
    syu, kyu, tyu = ([up_y(v, low) for v in vs[:slots]] for vs in (sy, kx, tx))
    ax = [jnp.maximum(v, w) for v, w in zip(sx, sxu, strict=True)]
    ay = [jnp.maximum(v, w) for v, w in zip(sy, syu, strict=True)]
    hx = [(kx[j] + kxu[j]) * (txu[j] - tx[j]) for j in five]
    hy = [(kx[j] + kyu[j]) * (tyu[j] - tx[j]) for j in range(slots)]

    def neighbours(f):
        u = [at(f, j) for j in five]
        fx = [physical(q, f, j, 0, z) for j in five]
        fy = [physical(q, f, j, 1, z) for j in range(slots)]
        return u, fx, fy, up_x(u, lane), up_x(fx, lane), [up_y(v, low) for v in u[:slots]], [up_y(v, low) for v in fy]

    def sides(f, u, fx, fy, ux, fux, uy, fuy):
        heat = lambda h: h if f == 4 else None
        gx = [face(u[j], ux[j], fx[j], fux[j], ax[j], heat(hx[j])) for j in five]
        gx[3] = jnp.where((lane >= LANES - BW) & (row == 7), gx[ghost], gx[3])
        d = [pltpu.roll(g, BW, 1) for g in gx]
        before = jnp.where(row == 0, d[ghost], pltpu.roll(d[3], 1, 0))
        dx = [jnp.where(lane >= BW, d[j], before if j == 0 else d[j - 1]) for j in range(4)] + [d[ghost]]
        gy = [face(u[j], uy[j], fy[j], fuy[j], ay[j], heat(hy[j])) for j in range(slots)]
        dy = [down_y(g, low) for g in gy]
        return [(gx[j] - dx[j]) + (gy[j] - dy[j]) for j in range(slots)]

    near = [neighbours(f) for f in range(6)]
    part = [sides(f, *near[f]) for f in range(6)]
    return {(f, j): part[f][j] for f in range(6) for j in range(slots)}


def raw_quantities(r, vx, vy, vz, p, s, k):
    t = p / r
    energy = p / (GAMMA - 1.0) + 0.5 * r * (vx * vx + vy * vy + vz * vz)
    return (r, r * vx, r * vy, r * vz, energy, r * s, vx, vy, vz, p, jnp.sqrt(GAMMA * t), t, k)


def store_all(ref, at, values):
    for j, quantities in enumerate(values):
        for i, value in enumerate(quantities):
            ref[(i,) + at + (j,)] = value


def inner_kernel(ext, q, total, token):
    token[...] = jnp.zeros(token.shape, jnp.float32)

    @pl.loop(0, 4, unroll=True)
    def _(z):
        found = []
        for j in range(5):
            rows = pl.ds(j, 8, stride=4) if j < 4 else pl.ds(32, 8)
            found.append(raw_quantities(*(ext[f, z, rows, :] for f in range(7))))
        store_all(q, (z,), found)

    @pl.loop(0, 4, unroll=True)
    def _(z):
        values = plane_divergence(q, z, 5)
        for (f, j), value in values.items():
            total[f, z, j] = value

    @pl.loop(0, 3, unroll=True)
    def _(z):
        faces = z_face_row(q, z, 5)
        lower = {(f, j): total[f, z, j] + value for (f, j), value in faces.items()}
        upper = {(f, j): total[f, z + 1, j] - value for (f, j), value in faces.items()}
        for (f, j), value in lower.items():
            total[f, z, j] = value
        for (f, j), value in upper.items():
            total[f, z + 1, j] = value


def outer_kernel(q, inner, rec_a, rec_slab, rec_b, total, edge_q, edge_total, token, rim, joined):
    even = lax.axis_index("near") % 2 == 0
    shape = (8, LANES)
    row = rows_of(shape)
    spread = lambda x: jnp.broadcast_to(x, shape)

    @pl.loop(0, 4, unroll=True)
    def _(z):
        for f in range(6):
            for j in range(5):
                total[f, z, j] = inner[f, z, j]

    token[...] = jnp.zeros(token.shape, jnp.float32)
    slab, pitch = rec_slab.shape[1] // 2, rec_a.shape[1] // 2
    for f in range(7):
        for z in range(2):
            at, to = 12 * z, pitch * z
            joined[f, to : to + slab, :] = rec_slab[f, slab * z : slab * z + slab, :]
            joined[f, to + slab : to + slab + 10, :] = rec_b[f, at : at + 10, :]
    for i in range(NQ):
        for j in range(5):
            rim[i, 2, j] = q[i, 0, j]
            rim[i, 3, j] = q[i, 3, j]
    for rec, base in ((rec_a, jnp.where(even, 4, 0)), (joined, jnp.where(even, 0, 4))):

        @pl.loop(0, 2, unroll=True)
        def _(z):
            found = []
            for j in range(5):
                if j < 4:
                    cells = (rec[f, pl.ds(36 * z + j, 8, stride=4), :] for f in range(7))
                else:
                    cells = (
                        jnp.where(row == 7, spread(rec[f, pl.ds(36 * z + 33, 1), :]), spread(rec[f, pl.ds(36 * z + 32, 1), :]))
                        for f in range(7)
                    )
                found.append(raw_quantities(*cells))
            store_all(rim, (base + z,), found)

    @pl.loop(0, 2, unroll=True)
    def _(e):
        z = 1 + 3 * e
        values = plane_divergence(rim, z, 5)
        for (f, j), value in values.items():
            edge_total[f, e, j] = value
        for j in range(5):
            for i, k in enumerate((0, 1, 2, 3, 4, 5, KAP)):
                edge_q[i, e, j] = rim[k, z, j]

    @pl.loop(0, 2, unroll=True)
    def _(e):
        below = z_face_row(rim, 3 * e, 5)
        above = z_face_row(rim, 3 * e + 1, 5)
        own = 3 * e
        change = {key: jnp.where(e == 0, -above[key], below[key]) for key in above}
        edge = {(f, j): edge_total[f, e, j] + (above[f, j] - below[f, j]) for f, j in above}
        done = {(f, j): inner[f, own, j] + value for (f, j), value in change.items()}
        for (f, j), value in edge.items():
            edge_total[f, e, j] = value
        for (f, j), value in done.items():
            total[f, own, j] = value


def second_kernel(base, total, edge_q, edge_total, arrival, peak, new_owner, out, q, zf, final, owner, sems):
    segment, segments = lax.axis_index("curve"), lax.axis_size("curve")
    shape = (8, LANES)
    lane, row = lanes_of(shape), rows_of(shape)
    first, last = segment == 0, segment == segments - 1
    fetch = pltpu.make_async_copy(new_owner, owner, sems.at[0])
    fetch.start()
    speed, top = jnp.max(peak[0:1, :]), jnp.max(peak[1:2, :])
    step = COURANT / (speed + 6.0 * top)

    def half_row(state, divergence, kap_at, source, target):
        half = [
            [state[f, source, j] - (0.5 * step) * divergence[f, source, j] for j in range(5)] for f in range(6)
        ]
        kap = [state[kap_at, source, j] for j in range(5)]
        for u in half + [kap]:
            edge = pltpu.roll(pltpu.roll(u[3], BW, 1), 1, 0)
            u[0] = jnp.where(last & (row == 6) & (lane < BW), edge, u[0])
            g = jnp.where((row == 0) & (lane < BW), u[0], u[4])
            g = jnp.where((row == 7) & (lane >= LANES - BW), u[3], g)
            u[4] = jnp.where(first & (row == 0) & (lane >= BW), pltpu.roll(g, LANES - BW, 1), g)
        found = []
        for j in range(5):
            r, mx, my, mz, e, s = (half[f][j] for f in range(6))
            inv = 1.0 / r
            vx, vy, vz = mx * inv, my * inv, mz * inv
            p = (GAMMA - 1.0) * (e - 0.5 * (mx * vx + my * vy + mz * vz))
            t = p * inv
            found.append((r, mx, my, mz, e, s, vx, vy, vz, p, jnp.sqrt(GAMMA * t), t, kap[j]))
        store_all(q, (target,), found)

    @pl.loop(0, 4, unroll=True)
    def _(z):
        half_row(base, total, KAP, z, z + 1)

    @pl.loop(0, 2, unroll=True)
    def _(e):
        half_row(edge_q, edge_total, 6, e, 5 * e)

    for key, value in z_face_row(q, 0, 4).items():
        zf[key] = value
    keep = (row < 6) | (arrival[...] > 0.5)
    final[:, 128:160, :] = jnp.zeros((6, 32, LANES), jnp.float32)

    @pl.loop(1, 5, unroll=True)
    def _(z):
        plane = plane_divergence(q, z, 4)
        faces = z_face_row(q, z, 4)
        done = {}
        for (f, j), value in faces.items():
            change = plane[f, j] + (value - zf[f, j])
            done[f, j] = 0.5 * (base[f, z - 1, j] + q[f, z, j]) - (0.25 * step) * change
        for (f, j), value in done.items():
            final[f, pl.ds(4 * j + z - 1, 8, stride=16), :] = jnp.where(keep, value, 0.0)
        for key, value in faces.items():
            zf[key] = value

    fetch.wait()
    start = jnp.where(owner[0] != segment, 32, 0)
    copy = pltpu.make_async_copy(final.at[:, pl.ds(pl.multiple_of(start, 32), 128), :], out, sems.at[1])
    copy.start()
    copy.wait()


def swap(x, partner):
    m, n = lax.axis_size("curve"), lax.axis_size("near")
    route = []
    for c in range(m):
        for i in range(n):
            to_c, to_i = partner(c, i)
            route.append((c * n + i, to_c * n + to_i))
    return lax.ppermute(x, ("curve", "near"), route)


def near_routes(n):
    routes = [lambda c, i: (c, i ^ 1), lambda c, i: (c, outer_partner(i, n))]
    reach = 4
    while reach < n:
        routes.append(lambda c, i, d=reach: (c, (i + d) % n))
        reach *= 2
    return routes


def curve_routes(m):
    routes, reach = [], 1
    while reach < m:
        if m % (2 * reach) == 0:
            routes.append(lambda c, i, d=reach: (c ^ d, i ^ 1))
        else:
            routes.append(lambda c, i, d=reach: ((c + d) % m, i ^ 1))
        reach *= 2
    return routes


def outer_partner(i, n):
    return ((i + 1) ^ 1) - 1 if 0 < i < n - 1 else n - 1 - i


def rows_view(x):
    lead, cells = x.shape[:-2], x.shape[-1]
    x = x.reshape(lead + (4, cells // LANES, LANES))
    return jnp.swapaxes(x, -3, -2).reshape(lead + (4 * (cells // LANES), LANES))


def kernel(body, name, ins, outs, scratch=(), us=0):
    cost = pl.CostEstimate(flops=int(us * 1e9), bytes_accessed=int(us * 3e6), transcendentals=0) if us else None
    return pl.pallas_call(
        body,
        out_shape=outs,
        in_specs=ins,
        out_specs=jax.tree.map(lambda _: VMEM, outs),
        scratch_shapes=scratch,
        compiler_params=PARAMS,
        cost_estimate=cost,
        name=name,
    )


def local(primitive, conductivity, new_owner):
    m, n = lax.axis_size("curve"), lax.axis_size("near")
    rows = primitive.shape[2] // LANES * 4
    in_hbm = lambda x: pltpu.with_memory_space_constraint(x, pltpu.HBM)
    prim, kappa, new_owner = in_hbm(rows_view(primitive)), in_hbm(rows_view(conductivity)), in_hbm(new_owner)
    hbm = pl.BlockSpec(memory_space=pltpu.HBM)

    own, peak, leaving = kernel(
        load_kernel,
        "load",
        [hbm, hbm, hbm],
        (f32(7, rows, LANES), f32(2, LANES), f32(8, LANES)),
        [pltpu.SMEM(new_owner.shape, jnp.int32), pltpu.SemaphoreType.DMA((3,))],
    )(prim, kappa, new_owner)

    side = lambda upper, name: kernel(functools.partial(side_kernel, upper), name, [VMEM] * 3, f32(7, 40, LANES))
    quantities, sums = f32(NQ, 4, 5, 8, LANES), f32(6, 4, 5, 8, LANES)
    routes = near_routes(n) + curve_routes(m)
    token = None
    for stage, route in enumerate(routes):
        if stage == DEP_C:
            rec_c = swap(side(True, "upper")(own, leaving, peak), lambda c, i: (c ^ 1, i))
        if stage == DEP_D:
            msg_d = side(False, "lower")(own, leaving, peak)
            rec_d = swap(msg_d, lambda c, i: (c, i ^ 1) if c in (0, m - 1) else (outer_partner(c, m), i))
        if stage == DEP_B:
            slab = kernel(slab_kernel, "slab", [VMEM] * 2, f32(7, rows // 2, LANES), us=COST["slab"])(own, peak)
            rec_slab = swap(slab, lambda c, i: (c, outer_partner(i, n)))
        if stage == DEP_S:
            ext, msg_a, msg_b, arrival, peak = kernel(
                spread_kernel,
                "spread",
                [VMEM] * 4,
                (f32(7, 4, 40, LANES), f32(7, 72, LANES), f32(7, 24, LANES), f32(8, LANES), f32(2, LANES)),
                us=COST["spread"],
            )(own, rec_c, rec_d, peak)
            rec_a = swap(msg_a, lambda c, i: (c, i ^ 1))
            rec_b = swap(msg_b, lambda c, i: (c, outer_partner(i, n)))
            q, inner, token = kernel(
                inner_kernel, "inner", [VMEM], (quantities, sums, f32(2, LANES)), us=COST["inner"]
            )(ext)
        peak = jnp.maximum(peak, swap(peak, route))
        if stage == DEP_I:
            peak = jnp.maximum(peak, token)
    total, edge_q, edge_total, token = kernel(
        outer_kernel,
        "outer",
        [VMEM] * 5,
        (sums, f32(7, 2, 5, 8, LANES), f32(6, 2, 5, 8, LANES), f32(2, LANES)),
        [pltpu.VMEM((NQ, 6, 5, 8, LANES), jnp.float32), pltpu.VMEM((7, 72, LANES), jnp.float32)],
        us=COST["outer"],
    )(q, inner, rec_a, rec_slab, rec_b)
    peak = jnp.maximum(peak, token)

    out = pl.pallas_call(
        second_kernel,
        out_shape=f32(6, rows + 32, LANES),
        in_specs=[VMEM] * 6 + [hbm],
        out_specs=hbm,
        scratch_shapes=[
            pltpu.VMEM((NQ, 6, 5, 8, LANES), jnp.float32),
            pltpu.VMEM((6, 4, 8, LANES), jnp.float32),
            pltpu.VMEM((6, rows + 64, LANES), jnp.float32),
            pltpu.SMEM(new_owner.shape, jnp.int32),
            pltpu.SemaphoreType.DMA((2,)),
        ],
        compiler_params=PARAMS,
        name="second_section",
    )(q, total, edge_q, edge_total, arrival, peak, new_owner)
    out = jnp.swapaxes(out.reshape(6, (rows + 32) // 4, 4, LANES), 1, 2)
    return out.reshape(1, 6, 4, (rows + 32) // 4 * LANES)


def solution(mesh):
    in_specs = (P(None, "near", "curve"), P("near", "curve"), P("curve"))
    out_specs = P("curve", None, "near", None)
    return jax.shard_map(local, mesh=mesh, in_specs=in_specs, out_specs=out_specs, check_vma=False)
```

```python
import functools

import jax
import jax.numpy as jnp
from jax import lax
from jax.experimental import pallas as pl
from jax.experimental.pallas import tpu as pltpu
from jax.sharding import PartitionSpec as P

BW = 32
LANES = 128
PLANES = LANES // BW
GAMMA = 1.4
COURANT = 0.8
COST = {"slab": 0, "spread": 1, "inner": 20, "outer": 20}
NQ = 13
VX, PR, SND, TMP, KAP = 6, 9, 10, 11, 12
VMEM = pl.BlockSpec(memory_space=pltpu.VMEM)
PARAMS = pltpu.CompilerParams(vmem_limit_bytes=24 * 1024 * 1024)


def f32(*shape):
    return jax.ShapeDtypeStruct(shape, jnp.float32)


def lanes_of(shape):
    return lax.broadcasted_iota(jnp.int32, shape, 1)


def rows_of(shape):
    return lax.broadcasted_iota(jnp.int32, shape, 0)


def load_kernel(prim, kappa, new_owner, own, peak, leaving, owner, sems):
    total = own.shape[1]
    copies = [
        pltpu.make_async_copy(prim, own.at[pl.ds(0, 6)], sems.at[0]),
        pltpu.make_async_copy(kappa, own.at[6], sems.at[1]),
        pltpu.make_async_copy(new_owner, owner, sems.at[2]),
    ]
    for copy in copies:
        copy.start()
    for copy in copies:
        copy.wait()
    speed = top = None
    for g in range(total // 8):
        r = pl.ds(8 * g, 8)
        sound = jnp.sqrt(GAMMA * own[4, r, :] / own[0, r, :])
        s = jnp.abs(own[1, r, :]) + jnp.abs(own[2, r, :]) + jnp.abs(own[3, r, :]) + 3.0 * sound
        speed = s if speed is None else jnp.maximum(speed, s)
        top = own[6, r, :] if top is None else jnp.maximum(top, own[6, r, :])
    speed, top = jnp.max(speed, axis=0, keepdims=True), jnp.max(top, axis=0, keepdims=True)
    halves = [jnp.maximum(v, pltpu.roll(v, LANES // 2, 1)) for v in (speed, top)]
    peak[...] = jnp.where(lanes_of((1, LANES)) < LANES // 2, *halves)
    leaves = (owner[0] != lax.axis_index("curve")).astype(jnp.float32)
    leaving[...] = jnp.full(leaving.shape, leaves, jnp.float32)


def side_kernel(upper_when_even, own, leaving, msg):
    even = lax.axis_index("curve") % 2 == 0
    box = jnp.logical_not(even) if upper_when_even else even
    total = own.shape[1]
    for g in range(5):
        length = 8 if g < 4 else 4
        first, last = pl.ds(8 * g, length), pl.ds(total - 36 + 8 * g, length)
        parts = [jnp.where(box, own[f, first, :], own[f, last, :]) for f in range(7)]
        for f in range(7):
            msg[f, first, :] = parts[f]
    for f in range(7):
        msg[f, 36:40, :] = leaving[0:4, :]


def slab_kernel(own, peak, msg, peaks):
    peaks[...] = jnp.broadcast_to(peak[...][None], peaks.shape)
    up = lax.axis_index("near") % 2 == 1
    groups = own.shape[1] // 32
    for f in range(7):
        parts = {}
        for z in range(2):
            for g in range(groups):
                upper, lower = (own[f, pl.ds(k + 32 * g, 8, stride=4), :] for k in (z + 2, z))
                parts[8 * (groups * z + g)] = jnp.where(up, upper, lower)
        for at, value in parts.items():
            msg[f, at : at + 8, :] = value


def spread_kernel(own, rec_c, rec_d, ext, msg_a, msg_b, arrival):
    segment, segments = lax.axis_index("curve"), lax.axis_size("curve")
    first, last = segment == 0, segment == segments - 1
    odd = segment % 2 == 1
    up = lax.axis_index("near") % 2 == 0
    groups = own.shape[1] // 32
    shape = (8, LANES)
    lane, row = lanes_of(shape), rows_of(shape)
    spread = lambda x: jnp.broadcast_to(x, shape)
    arrival[...] = jnp.where(last, 0.0, spread(jnp.where(odd, rec_d[0, 36:37, :], rec_c[0, 36:37, :])))
    for f in range(7):
        out = []
        for z in range(4):
            cells = [own[f, pl.ds(z + 32 * g, 8, stride=4), :] for g in range(groups)]
            at = pl.ds(z, 8, stride=4)
            box = jnp.where(odd, rec_d[f, at, :], rec_c[f, at, :])
            beyond = spread(jnp.where(odd, rec_d[f, 32 + z : 33 + z, :], rec_c[f, 32 + z : 33 + z, :]))
            behind = spread(jnp.where(odd, rec_c[f, 32 + z : 33 + z, :], rec_d[f, 32 + z : 33 + z, :]))
            edge = pltpu.roll(spread(cells[-1][7:8]), BW, 1)
            box = jnp.where(last, edge, box)
            start, end = spread(cells[0][0:1]), spread(box[7:8])
            behind = jnp.where(first, pltpu.roll(start, LANES - BW, 1), behind)
            low_side = jnp.where(lane < BW, start, behind)
            high_side = jnp.where(lane >= LANES - BW, end, beyond)
            out.append(cells + [box, jnp.where(row == 7, high_side, low_side)])
        for z in range(4):
            for g, value in enumerate(out[z]):
                ext[f, z, 8 * g : 8 * g + 8, :] = value
        for msg, ahead, pitch, begin in ((msg_a, up, 36, 0), (msg_b, jnp.logical_not(up), 12, groups)):
            for z in range(2):
                for g in range(begin, groups + 2):
                    value = jnp.where(ahead, out[z + 2][g], out[z][g])
                    at = pitch * z + 8 * (g - begin)
                    if g < groups + 1:
                        msg[f, at : at + 8, :] = value
                    else:
                        msg[f, at : at + 1, :] = value[0:1]
                        msg[f, at + 1 : at + 2, :] = value[7:8]


def up_x(q, lane):
    w = [pltpu.roll(v, LANES - BW, 1) for v in q[:4]]
    w.append(pltpu.roll(w[0], 7, 0))
    return [jnp.where(lane < LANES - BW, w[j], w[j + 1]) for j in range(4)] + [pltpu.roll(q[4], LANES - BW, 1)]


def up_y(v, low):
    return jnp.where(low == BW - 1, pltpu.roll(v, BW - 1, 1), pltpu.roll(v, LANES - 1, 1))


def down_y(v, low):
    return jnp.where(low == 0, pltpu.roll(v, LANES - BW + 1, 1), pltpu.roll(v, 1, 1))


def face(lower_u, upper_u, lower_f, upper_f, speed, heat):
    out = (lower_f + upper_f) - speed * (upper_u - lower_u)
    return out if heat is None else out - heat


def z_face_row(q, z, slots):
    speed, heat = [], []
    for j in range(slots):
        s0 = jnp.abs(q[VX + 2, z, j]) + q[SND, z, j]
        s1 = jnp.abs(q[VX + 2, z + 1, j]) + q[SND, z + 1, j]
        speed.append(jnp.maximum(s0, s1))
        heat.append((q[KAP, z, j] + q[KAP, z + 1, j]) * (q[TMP, z + 1, j] - q[TMP, z, j]))
    return {
        (f, j): face(
            q[f, z, j],
            q[f, z + 1, j],
            physical(q, f, j, 2, z),
            physical(q, f, j, 2, z + 1),
            speed[j],
            heat[j] if f == 4 else None,
        )
        for f in range(6)
        for j in range(slots)
    }


def physical(q, f, j, k, z):
    if f == 0:
        return q[1 + k, z, j]
    v = q[VX + k, z, j]
    if f == 4:
        return (q[4, z, j] + q[PR, z, j]) * v
    out = q[f, z, j] * v
    return out + q[PR, z, j] if f == 1 + k else out


def plane_divergence(q, z, slots):
    shape = (8, LANES)
    lane, row = lanes_of(shape), rows_of(shape)
    low = lane & (BW - 1)
    ghost = 4
    five = range(5)
    at = lambda i, j: q[i, z, j]
    sx = [jnp.abs(at(VX, j)) + at(SND, j) for j in five]
    sy = [jnp.abs(at(VX + 1, j)) + at(SND, j) for j in range(slots)]
    kx, tx = [at(KAP, j) for j in five], [at(TMP, j) for j in five]
    sxu, kxu, txu = up_x(sx, lane), up_x(kx, lane), up_x(tx, lane)
    syu, kyu, tyu = ([up_y(v, low) for v in vs[:slots]] for vs in (sy, kx, tx))
    ax = [jnp.maximum(v, w) for v, w in zip(sx, sxu, strict=True)]
    ay = [jnp.maximum(v, w) for v, w in zip(sy, syu, strict=True)]
    hx = [(kx[j] + kxu[j]) * (txu[j] - tx[j]) for j in five]
    hy = [(kx[j] + kyu[j]) * (tyu[j] - tx[j]) for j in range(slots)]

    def neighbours(f):
        u = [at(f, j) for j in five]
        fx = [physical(q, f, j, 0, z) for j in five]
        fy = [physical(q, f, j, 1, z) for j in range(slots)]
        return u, fx, fy, up_x(u, lane), up_x(fx, lane), [up_y(v, low) for v in u[:slots]], [up_y(v, low) for v in fy]

    def sides(f, u, fx, fy, ux, fux, uy, fuy):
        heat = lambda h: h if f == 4 else None
        gx = [face(u[j], ux[j], fx[j], fux[j], ax[j], heat(hx[j])) for j in five]
        gx[3] = jnp.where((lane >= LANES - BW) & (row == 7), gx[ghost], gx[3])
        d = [pltpu.roll(g, BW, 1) for g in gx]
        before = jnp.where(row == 0, d[ghost], pltpu.roll(d[3], 1, 0))
        dx = [jnp.where(lane >= BW, d[j], before if j == 0 else d[j - 1]) for j in range(4)] + [d[ghost]]
        gy = [face(u[j], uy[j], fy[j], fuy[j], ay[j], heat(hy[j])) for j in range(slots)]
        dy = [down_y(g, low) for g in gy]
        return [(gx[j] - dx[j]) + (gy[j] - dy[j]) for j in range(slots)]

    near = [neighbours(f) for f in range(6)]
    part = [sides(f, *near[f]) for f in range(6)]
    return {(f, j): part[f][j] for f in range(6) for j in range(slots)}


def raw_quantities(r, vx, vy, vz, p, s, k):
    t = p / r
    energy = p / (GAMMA - 1.0) + 0.5 * r * (vx * vx + vy * vy + vz * vz)
    return (r, r * vx, r * vy, r * vz, energy, r * s, vx, vy, vz, p, jnp.sqrt(GAMMA * t), t, k)


def store_all(ref, at, values):
    for j, quantities in enumerate(values):
        for i, value in enumerate(quantities):
            ref[(i,) + at + (j,)] = value


def inner_kernel(ext, order, q, total):
    @pl.loop(0, 4, unroll=True)
    def _(z):
        found = []
        for j in range(5):
            rows = pl.ds(j, 8, stride=4) if j < 4 else pl.ds(32, 8)
            found.append(raw_quantities(*(ext[f, z, rows, :] for f in range(7))))
        store_all(q, (z,), found)

    @pl.loop(0, 4, unroll=True)
    def _(z):
        values = plane_divergence(q, z, 5)
        for (f, j), value in values.items():
            total[f, z, j] = value

    @pl.loop(0, 3, unroll=True)
    def _(z):
        faces = z_face_row(q, z, 5)
        lower = {(f, j): total[f, z, j] + value for (f, j), value in faces.items()}
        upper = {(f, j): total[f, z + 1, j] - value for (f, j), value in faces.items()}
        for (f, j), value in lower.items():
            total[f, z, j] = value
        for (f, j), value in upper.items():
            total[f, z + 1, j] = value


def outer_kernel(q, inner, rec_a, rec_slab, rec_b, total, edge_q, edge_total, rim, joined):
    even = lax.axis_index("near") % 2 == 0
    shape = (8, LANES)
    row = rows_of(shape)
    spread = lambda x: jnp.broadcast_to(x, shape)

    @pl.loop(0, 4, unroll=True)
    def _(z):
        for f in range(6):
            for j in range(5):
                total[f, z, j] = inner[f, z, j]

    slab, pitch = rec_slab.shape[1] // 2, rec_a.shape[1] // 2
    for f in range(7):
        for z in range(2):
            at, to = 12 * z, pitch * z
            joined[f, to : to + slab, :] = rec_slab[f, slab * z : slab * z + slab, :]
            joined[f, to + slab : to + slab + 10, :] = rec_b[f, at : at + 10, :]
    for i in range(NQ):
        for j in range(5):
            rim[i, 2, j] = q[i, 0, j]
            rim[i, 3, j] = q[i, 3, j]
    for rec, base in ((rec_a, jnp.where(even, 4, 0)), (joined, jnp.where(even, 0, 4))):

        @pl.loop(0, 2, unroll=True)
        def _(z):
            found = []
            for j in range(5):
                if j < 4:
                    cells = (rec[f, pl.ds(36 * z + j, 8, stride=4), :] for f in range(7))
                else:
                    cells = (
                        jnp.where(row == 7, spread(rec[f, pl.ds(36 * z + 33, 1), :]), spread(rec[f, pl.ds(36 * z + 32, 1), :]))
                        for f in range(7)
                    )
                found.append(raw_quantities(*cells))
            store_all(rim, (base + z,), found)

    @pl.loop(0, 2, unroll=True)
    def _(e):
        z = 1 + 3 * e
        values = plane_divergence(rim, z, 5)
        for (f, j), value in values.items():
            edge_total[f, e, j] = value
        for j in range(5):
            for i, k in enumerate((0, 1, 2, 3, 4, 5, KAP)):
                edge_q[i, e, j] = rim[k, z, j]

    @pl.loop(0, 2, unroll=True)
    def _(e):
        below = z_face_row(rim, 3 * e, 5)
        above = z_face_row(rim, 3 * e + 1, 5)
        own = 3 * e
        change = {key: jnp.where(e == 0, -above[key], below[key]) for key in above}
        edge = {(f, j): edge_total[f, e, j] + (above[f, j] - below[f, j]) for f, j in above}
        done = {(f, j): inner[f, own, j] + value for (f, j), value in change.items()}
        for (f, j), value in edge.items():
            edge_total[f, e, j] = value
        for (f, j), value in done.items():
            total[f, own, j] = value


def second_kernel(base, total, edge_q, edge_total, arrival, peak, new_owner, out, q, zf, final, owner, sems):
    segment, segments = lax.axis_index("curve"), lax.axis_size("curve")
    shape = (8, LANES)
    lane, row = lanes_of(shape), rows_of(shape)
    first, last = segment == 0, segment == segments - 1
    fetch = pltpu.make_async_copy(new_owner, owner, sems.at[0])
    fetch.start()
    peaks = jnp.max(peak[...], axis=0)
    half_lanes = lanes_of((1, LANES)) < LANES // 2
    speed, top = jnp.max(jnp.where(half_lanes, peaks, 0.0)), jnp.max(jnp.where(half_lanes, 0.0, peaks))
    step = COURANT / (speed + 6.0 * top)

    def half_row(state, divergence, kap_at, source, target):
        half = [
            [state[f, source, j] - (0.5 * step) * divergence[f, source, j] for j in range(5)] for f in range(6)
        ]
        kap = [state[kap_at, source, j] for j in range(5)]
        for u in half + [kap]:
            edge = pltpu.roll(pltpu.roll(u[3], BW, 1), 1, 0)
            u[0] = jnp.where(last & (row == 6) & (lane < BW), edge, u[0])
            g = jnp.where((row == 0) & (lane < BW), u[0], u[4])
            g = jnp.where((row == 7) & (lane >= LANES - BW), u[3], g)
            u[4] = jnp.where(first & (row == 0) & (lane >= BW), pltpu.roll(g, LANES - BW, 1), g)
        found = []
        for j in range(5):
            r, mx, my, mz, e, s = (half[f][j] for f in range(6))
            inv = 1.0 / r
            vx, vy, vz = mx * inv, my * inv, mz * inv
            p = (GAMMA - 1.0) * (e - 0.5 * (mx * vx + my * vy + mz * vz))
            t = p * inv
            found.append((r, mx, my, mz, e, s, vx, vy, vz, p, jnp.sqrt(GAMMA * t), t, kap[j]))
        store_all(q, (target,), found)

    @pl.loop(0, 4, unroll=True)
    def _(z):
        half_row(base, total, KAP, z, z + 1)

    @pl.loop(0, 2, unroll=True)
    def _(e):
        half_row(edge_q, edge_total, 6, e, 5 * e)

    for key, value in z_face_row(q, 0, 4).items():
        zf[key] = value
    keep = (row < 6) | (arrival[...] > 0.5)
    final[:, 128:160, :] = jnp.zeros((6, 32, LANES), jnp.float32)

    @pl.loop(1, 5, unroll=True)
    def _(z):
        plane = plane_divergence(q, z, 4)
        faces = z_face_row(q, z, 4)
        done = {}
        for (f, j), value in faces.items():
            change = plane[f, j] + (value - zf[f, j])
            done[f, j] = 0.5 * (base[f, z - 1, j] + q[f, z, j]) - (0.25 * step) * change
        for (f, j), value in done.items():
            final[f, pl.ds(4 * j + z - 1, 8, stride=16), :] = jnp.where(keep, value, 0.0)
        for key, value in faces.items():
            zf[key] = value

    fetch.wait()
    start = jnp.where(owner[0] != segment, 32, 0)
    copy = pltpu.make_async_copy(final.at[:, pl.ds(pl.multiple_of(start, 32), 128), :], out, sems.at[1])
    copy.start()
    copy.wait()


def swap(x, partner):
    m, n = lax.axis_size("curve"), lax.axis_size("near")
    route = []
    for c in range(m):
        for i in range(n):
            to_c, to_i = partner(c, i)
            route.append((c * n + i, to_c * n + to_i))
    return lax.ppermute(x, ("curve", "near"), route)


def outer_partner(i, n):
    return ((i + 1) ^ 1) - 1 if 0 < i < n - 1 else n - 1 - i


def rows_view(x):
    lead, cells = x.shape[:-2], x.shape[-1]
    x = x.reshape(lead + (4, cells // LANES, LANES))
    return jnp.swapaxes(x, -3, -2).reshape(lead + (4 * (cells // LANES), LANES))


def kernel(body, name, ins, outs, scratch=(), us=0):
    cost = pl.CostEstimate(flops=int(us * 1e9), bytes_accessed=int(us * 3e6), transcendentals=0) if us else None
    return pl.pallas_call(
        body,
        out_shape=outs,
        in_specs=ins,
        out_specs=jax.tree.map(lambda _: VMEM, outs),
        scratch_shapes=scratch,
        compiler_params=PARAMS,
        cost_estimate=cost,
        name=name,
    )


def local(primitive, conductivity, new_owner):
    m, n = lax.axis_size("curve"), lax.axis_size("near")
    rows = primitive.shape[2] // LANES * 4
    in_hbm = lambda x: pltpu.with_memory_space_constraint(x, pltpu.HBM)
    prim, kappa, new_owner = in_hbm(rows_view(primitive)), in_hbm(rows_view(conductivity)), in_hbm(new_owner)
    hbm = pl.BlockSpec(memory_space=pltpu.HBM)

    own, peak, leaving = kernel(
        load_kernel,
        "load",
        [hbm, hbm, hbm],
        (f32(7, rows, LANES), f32(1, LANES), f32(8, LANES)),
        [pltpu.SMEM(new_owner.shape, jnp.int32), pltpu.SemaphoreType.DMA((3,))],
    )(prim, kappa, new_owner)

    side = lambda upper, name: kernel(functools.partial(side_kernel, upper), name, [VMEM] * 2, f32(7, 40, LANES))
    quantities, sums = f32(NQ, 4, 5, 8, LANES), f32(6, 4, 5, 8, LANES)
    rec_c = swap(side(True, "upper")(own, leaving), lambda c, i: (c ^ 1, i))
    msg_d = side(False, "lower")(own, leaving)
    rec_d = swap(msg_d, lambda c, i: (c, i ^ 1) if c in (0, m - 1) else (outer_partner(c, m), i))
    slab, peak = kernel(
        slab_kernel, "slab", [VMEM] * 2, (f32(7, rows // 2, LANES), f32(m * n, 1, LANES)), us=COST["slab"]
    )(own, peak)
    rec_slab = swap(slab, lambda c, i: (c, outer_partner(i, n)))
    peak = lax.all_to_all(peak, ("curve", "near"), 0, 0, tiled=True)
    ext, msg_a, msg_b, arrival = kernel(
        spread_kernel,
        "spread",
        [VMEM] * 3,
        (f32(7, 4, 40, LANES), f32(7, 72, LANES), f32(7, 24, LANES), f32(8, LANES)),
        us=COST["spread"],
    )(own, rec_c, rec_d)
    rec_a = swap(msg_a, lambda c, i: (c, i ^ 1))
    rec_b = swap(msg_b, lambda c, i: (c, outer_partner(i, n)))
    q, inner = kernel(inner_kernel, "inner", [VMEM] * 2, (quantities, sums), us=COST["inner"])(ext, rec_slab)
    total, edge_q, edge_total = kernel(
        outer_kernel,
        "outer",
        [VMEM] * 5,
        (sums, f32(7, 2, 5, 8, LANES), f32(6, 2, 5, 8, LANES)),
        [pltpu.VMEM((NQ, 6, 5, 8, LANES), jnp.float32), pltpu.VMEM((7, 72, LANES), jnp.float32)],
        us=COST["outer"],
    )(q, inner, rec_a, rec_slab, rec_b)

    out = pl.pallas_call(
        second_kernel,
        out_shape=f32(6, rows + 32, LANES),
        in_specs=[VMEM] * 6 + [hbm],
        out_specs=hbm,
        scratch_shapes=[
            pltpu.VMEM((NQ, 6, 5, 8, LANES), jnp.float32),
            pltpu.VMEM((6, 4, 8, LANES), jnp.float32),
            pltpu.VMEM((6, rows + 64, LANES), jnp.float32),
            pltpu.SMEM(new_owner.shape, jnp.int32),
            pltpu.SemaphoreType.DMA((2,)),
        ],
        compiler_params=PARAMS,
        name="second_section",
    )(q, total, edge_q, edge_total, arrival, peak, new_owner)
    out = jnp.swapaxes(out.reshape(6, (rows + 32) // 4, 4, LANES), 1, 2)
    return out.reshape(1, 6, 4, (rows + 32) // 4 * LANES)


def solution(mesh):
    in_specs = (P(None, "near", "curve"), P("near", "curve"), P("curve"))
    out_specs = P("curve", None, "near", None)
    return jax.shard_map(local, mesh=mesh, in_specs=in_specs, out_specs=out_specs, check_vma=False)
```

```python
import functools

import jax
import jax.numpy as jnp
from jax import lax
from jax.experimental import pallas as pl
from jax.experimental.pallas import tpu as pltpu
from jax.sharding import PartitionSpec as P

BW = 32
LANES = 128
PLANES = LANES // BW
GAMMA = 1.4
COURANT = 0.8
COST = {"spread": 0.3, "inner": 20, "outer": 20}
NQ = 13
VX, PR, SND, TMP, KAP = 6, 9, 10, 11, 12
VMEM = pl.BlockSpec(memory_space=pltpu.VMEM)
PARAMS = pltpu.CompilerParams(vmem_limit_bytes=24 * 1024 * 1024)


def f32(*shape):
    return jax.ShapeDtypeStruct(shape, jnp.float32)


def lanes_of(shape):
    return lax.broadcasted_iota(jnp.int32, shape, 1)


def rows_of(shape):
    return lax.broadcasted_iota(jnp.int32, shape, 0)


def load_kernel(prim, kappa, new_owner, own, msg_c, msg_d, slab, peak, owner, sems):
    segment = lax.axis_index("curve")
    even, up = segment % 2 == 0, lax.axis_index("near") % 2 == 1
    total = own.shape[1]
    groups = total // 32
    copies = [
        pltpu.make_async_copy(prim, own.at[pl.ds(0, 6)], sems.at[0]),
        pltpu.make_async_copy(kappa, own.at[6], sems.at[1]),
        pltpu.make_async_copy(new_owner, owner, sems.at[2]),
    ]
    for copy in copies:
        copy.start()
    for copy in copies:
        copy.wait()
    speed = top = None
    for g in range(total // 8):
        r = pl.ds(8 * g, 8)
        sound = jnp.sqrt(GAMMA * own[4, r, :] / own[0, r, :])
        s = jnp.abs(own[1, r, :]) + jnp.abs(own[2, r, :]) + jnp.abs(own[3, r, :]) + 3.0 * sound
        speed = s if speed is None else jnp.maximum(speed, s)
        top = own[6, r, :] if top is None else jnp.maximum(top, own[6, r, :])
    speed, top = jnp.max(speed, axis=0, keepdims=True), jnp.max(top, axis=0, keepdims=True)
    halves = [jnp.maximum(v, pltpu.roll(v, LANES // 2, 1)) for v in (speed, top)]
    peak[...] = jnp.where(lanes_of((1, LANES)) < LANES // 2, *halves)
    leaves = jnp.full((2, LANES), (owner[0] != segment).astype(jnp.float32), jnp.float32)
    low_half = lanes_of((1, LANES)) < LANES // 2
    swapped = lambda x: pltpu.roll(x, LANES // 2, 1)
    for msg, box in ((msg_c, jnp.logical_not(even)), (msg_d, even)):
        for f in range(7):
            parts = [own[f, 8 * g : 8 * g + 8, :] for g in range(4)]
            for z in (0, 2):
                first, second = (own[f, k : k + 1, :] for k in (32 + z, 33 + z))
                ahead = jnp.where(low_half, first, swapped(second))
                first, second = (own[f, k : k + 1, :] for k in (total - 4 + z, total - 3 + z))
                parts.append(jnp.where(box, ahead, jnp.where(low_half, swapped(first), second)))
            at = 34 * f
            for part in parts:
                msg[at : at + part.shape[0], :] = part
                at += part.shape[0]
        msg[238:240, :] = leaves
    for f in range(7):
        parts = {}
        for z in range(2):
            for g in range(groups):
                upper, lower = (own[f, pl.ds(k + 32 * g, 8, stride=4), :] for k in (z + 2, z))
                parts[8 * (groups * z + g)] = jnp.where(up, upper, lower)
        for at, value in parts.items():
            slab[f, at : at + 8, :] = value


def copies_kernel(peak, peaks):
    peaks[...] = jnp.broadcast_to(peak[...][None], peaks.shape)


def spread_kernel(own, rec_c, rec_d, ext, msg_a, msg_b, arrival):
    segment, segments = lax.axis_index("curve"), lax.axis_size("curve")
    first, last = segment == 0, segment == segments - 1
    odd = segment % 2 == 1
    up = lax.axis_index("near") % 2 == 0
    groups = own.shape[1] // 32
    shape = (8, LANES)
    lane, row = lanes_of(shape), rows_of(shape)
    spread = lambda x: jnp.broadcast_to(x, shape)
    arrival[...] = jnp.where(last, 0.0, spread(jnp.where(odd, rec_d[238:239, :], rec_c[238:239, :])))
    for f in range(7):
        out = []
        for z in range(4):
            cells = [own[f, pl.ds(z + 32 * g, 8, stride=4), :] for g in range(groups)]
            at = pl.ds(34 * f + z, 8, stride=4)
            box = jnp.where(odd, rec_d[at, :], rec_c[at, :])
            at = pl.ds(34 * f + 32 + z // 2, 1)
            beyond = jnp.where(odd, rec_d[at, :], rec_c[at, :])
            behind = jnp.where(odd, rec_c[at, :], rec_d[at, :])
            if z % 2:
                beyond = pltpu.roll(beyond, LANES // 2, 1)
            else:
                behind = pltpu.roll(behind, LANES // 2, 1)
            beyond, behind = spread(beyond), spread(behind)
            edge = pltpu.roll(spread(cells[-1][7:8]), BW, 1)
            box = jnp.where(last, edge, box)
            start, end = spread(cells[0][0:1]), spread(box[7:8])
            behind = jnp.where(first, pltpu.roll(start, LANES - BW, 1), behind)
            low_side = jnp.where(lane < BW, start, behind)
            high_side = jnp.where(lane >= LANES - BW, end, beyond)
            out.append(cells + [box, jnp.where(row == 7, high_side, low_side)])
        for z in range(4):
            for g, value in enumerate(out[z]):
                ext[f, z, 8 * g : 8 * g + 8, :] = value
        for z in range(2):
            for g in range(groups + 2):
                value = jnp.where(up, out[z + 2][g], out[z][g])
                at = 36 * z + 8 * g
                if g < groups + 1:
                    msg_a[f, at : at + 8, :] = value
                else:
                    msg_a[f, at : at + 1, :] = value[0:1]
                    msg_a[f, at + 1 : at + 2, :] = value[7:8]
            at = 18 * f + 8 * z
            msg_b[at : at + 8, :] = jnp.where(up, out[z][groups], out[z + 2][groups])
        value = jnp.where(up, out[0][groups + 1], out[3][groups + 1])
        msg_b[18 * f + 16 : 18 * f + 17, :] = value[0:1]
        msg_b[18 * f + 17 : 18 * f + 18, :] = value[7:8]
    msg_b[126:128, :] = jnp.zeros((2, LANES), jnp.float32)


def up_x(q, lane):
    w = [pltpu.roll(v, LANES - BW, 1) for v in q[:4]]
    w.append(pltpu.roll(w[0], 7, 0))
    return [jnp.where(lane < LANES - BW, w[j], w[j + 1]) for j in range(4)] + [pltpu.roll(q[4], LANES - BW, 1)]


def up_y(v, low):
    return jnp.where(low == BW - 1, pltpu.roll(v, BW - 1, 1), pltpu.roll(v, LANES - 1, 1))


def down_y(v, low):
    return jnp.where(low == 0, pltpu.roll(v, LANES - BW + 1, 1), pltpu.roll(v, 1, 1))


def face(lower_u, upper_u, lower_f, upper_f, speed, heat):
    out = (lower_f + upper_f) - speed * (upper_u - lower_u)
    return out if heat is None else out - heat


def z_face_row(q, z, slots):
    speed, heat = [], []
    for j in range(slots):
        s0 = jnp.abs(q[VX + 2, z, j]) + q[SND, z, j]
        s1 = jnp.abs(q[VX + 2, z + 1, j]) + q[SND, z + 1, j]
        speed.append(jnp.maximum(s0, s1))
        heat.append((q[KAP, z, j] + q[KAP, z + 1, j]) * (q[TMP, z + 1, j] - q[TMP, z, j]))
    return {
        (f, j): face(
            q[f, z, j],
            q[f, z + 1, j],
            physical(q, f, j, 2, z),
            physical(q, f, j, 2, z + 1),
            speed[j],
            heat[j] if f == 4 else None,
        )
        for f in range(6)
        for j in range(slots)
    }


def physical(q, f, j, k, z):
    if f == 0:
        return q[1 + k, z, j]
    v = q[VX + k, z, j]
    if f == 4:
        return (q[4, z, j] + q[PR, z, j]) * v
    out = q[f, z, j] * v
    return out + q[PR, z, j] if f == 1 + k else out


def plane_divergence(q, z, slots):
    shape = (8, LANES)
    lane, row = lanes_of(shape), rows_of(shape)
    low = lane & (BW - 1)
    ghost = 4
    five = range(5)
    at = lambda i, j: q[i, z, j]
    sx = [jnp.abs(at(VX, j)) + at(SND, j) for j in five]
    sy = [jnp.abs(at(VX + 1, j)) + at(SND, j) for j in range(slots)]
    kx, tx = [at(KAP, j) for j in five], [at(TMP, j) for j in five]
    sxu, kxu, txu = up_x(sx, lane), up_x(kx, lane), up_x(tx, lane)
    syu, kyu, tyu = ([up_y(v, low) for v in vs[:slots]] for vs in (sy, kx, tx))
    ax = [jnp.maximum(v, w) for v, w in zip(sx, sxu, strict=True)]
    ay = [jnp.maximum(v, w) for v, w in zip(sy, syu, strict=True)]
    hx = [(kx[j] + kxu[j]) * (txu[j] - tx[j]) for j in five]
    hy = [(kx[j] + kyu[j]) * (tyu[j] - tx[j]) for j in range(slots)]

    def neighbours(f):
        u = [at(f, j) for j in five]
        fx = [physical(q, f, j, 0, z) for j in five]
        fy = [physical(q, f, j, 1, z) for j in range(slots)]
        return u, fx, fy, up_x(u, lane), up_x(fx, lane), [up_y(v, low) for v in u[:slots]], [up_y(v, low) for v in fy]

    def sides(f, u, fx, fy, ux, fux, uy, fuy):
        heat = lambda h: h if f == 4 else None
        gx = [face(u[j], ux[j], fx[j], fux[j], ax[j], heat(hx[j])) for j in five]
        gx[3] = jnp.where((lane >= LANES - BW) & (row == 7), gx[ghost], gx[3])
        d = [pltpu.roll(g, BW, 1) for g in gx]
        before = jnp.where(row == 0, d[ghost], pltpu.roll(d[3], 1, 0))
        dx = [jnp.where(lane >= BW, d[j], before if j == 0 else d[j - 1]) for j in range(4)] + [d[ghost]]
        gy = [face(u[j], uy[j], fy[j], fuy[j], ay[j], heat(hy[j])) for j in range(slots)]
        dy = [down_y(g, low) for g in gy]
        return [(gx[j] - dx[j]) + (gy[j] - dy[j]) for j in range(slots)]

    near = [neighbours(f) for f in range(6)]
    part = [sides(f, *near[f]) for f in range(6)]
    return {(f, j): part[f][j] for f in range(6) for j in range(slots)}


def raw_quantities(r, vx, vy, vz, p, s, k):
    t = p / r
    energy = p / (GAMMA - 1.0) + 0.5 * r * (vx * vx + vy * vy + vz * vz)
    return (r, r * vx, r * vy, r * vz, energy, r * s, vx, vy, vz, p, jnp.sqrt(GAMMA * t), t, k)


def state_quantities(r, mx, my, mz, e, s, k):
    inv = 1.0 / r
    vx, vy, vz = mx * inv, my * inv, mz * inv
    p = (GAMMA - 1.0) * (e - 0.5 * (mx * vx + my * vy + mz * vz))
    t = p * inv
    return (r, mx, my, mz, e, s, vx, vy, vz, p, jnp.sqrt(GAMMA * t), t, k)


def store_all(ref, at, values):
    for j, quantities in enumerate(values):
        for i, value in enumerate(quantities):
            ref[(i,) + at + (j,)] = value


def inner_kernel(ext, order, q, total):
    @pl.loop(0, 4, unroll=True)
    def _(z):
        found = []
        for j in range(5):
            rows = pl.ds(j, 8, stride=4) if j < 4 else pl.ds(32, 8)
            found.append(raw_quantities(*(ext[f, z, rows, :] for f in range(7))))
        store_all(q, (z,), found)

    @pl.loop(0, 4, unroll=True)
    def _(z):
        values = plane_divergence(q, z, 5)
        for (f, j), value in values.items():
            total[f, z, j] = value

    @pl.loop(0, 3, unroll=True)
    def _(z):
        faces = z_face_row(q, z, 5)
        lower = {(f, j): total[f, z, j] + value for (f, j), value in faces.items()}
        upper = {(f, j): total[f, z + 1, j] - value for (f, j), value in faces.items()}
        for (f, j), value in lower.items():
            total[f, z, j] = value
        for (f, j), value in upper.items():
            total[f, z + 1, j] = value


def rim_kernel(with_a, q, inner, *refs):
    *received, edge_q, edge_total, own_total, rim = refs[:-1] if not with_a else refs
    even = lax.axis_index("near") % 2 == 0
    above_own = even if with_a else jnp.logical_not(even)
    start, own = jnp.where(above_own, 1, 0), jnp.where(above_own, 3, 0)
    row = rows_of((8, LANES))
    spread = lambda x: jnp.broadcast_to(x, (8, LANES))
    if with_a:
        (rows,) = received
    else:
        rows, (rec_slab, rec_box) = refs[-1], received
        slab = rec_slab.shape[1] // 2
        for f in range(7):
            for z in range(2):
                at, box = 36 * z, 18 * f + 8 * z
                rows[f, at : at + slab, :] = rec_slab[f, slab * z : slab * z + slab, :]
                rows[f, at + slab : at + slab + 8, :] = rec_box[box : box + 8, :]
                rows[f, at + slab + 8 : at + slab + 10, :] = rec_box[18 * f + 16 : 18 * f + 18, :]
    kept = [[q[i, own, j] for i in range(NQ)] for j in range(5)]
    store_all(rim, (jnp.where(above_own, 0, 2),), kept)
    for z in range(2):
        found = []
        for j in range(5):
            if j < 4:
                cells = (rows[f, pl.ds(36 * z + j, 8, stride=4), :] for f in range(7))
            else:
                at = 36 * z + 32
                cells = (
                    jnp.where(row == 7, spread(rows[f, at + 1 : at + 2, :]), spread(rows[f, at : at + 1, :]))
                    for f in range(7)
                )
            found.append(raw_quantities(*cells))
        store_all(rim, (start + z,), found)
    plane = plane_divergence(rim, 1, 4)
    below, above = z_face_row(rim, 0, 5), z_face_row(rim, 1, 5)
    change = {key: jnp.where(above_own, below[key], -above[key]) for key in above}
    done = {(f, j): inner[f, own, j] + value for (f, j), value in change.items()}
    for (f, j), value in plane.items():
        edge_total[f, j] = value + (above[f, j] - below[f, j])
    for (f, j), value in done.items():
        own_total[f, j] = value
    for j in range(4):
        for i, k in enumerate((0, 1, 2, 3, 4, 5, KAP)):
            edge_q[i, j] = rim[k, 1, j]


def second_kernel(
    base, total, edge_a, change_a, own_a, edge_b, change_b, own_b, arrival, peak, new_owner, out, q, zf, final, owner, sems
):
    segment, segments = lax.axis_index("curve"), lax.axis_size("curve")
    shape = (8, LANES)
    lane, row = lanes_of(shape), rows_of(shape)
    first, last = segment == 0, segment == segments - 1
    fetch = pltpu.make_async_copy(new_owner, owner, sems.at[0])
    fetch.start()
    peaks = jnp.max(peak[...], axis=0)
    half_lanes = lanes_of((1, LANES)) < LANES // 2
    speed, top = jnp.max(jnp.where(half_lanes, peaks, 0.0)), jnp.max(jnp.where(half_lanes, 0.0, peaks))
    step = COURANT / (speed + 6.0 * top)

    even = lax.axis_index("near") % 2 == 0

    def own_row(z):
        if z in (0, 3):
            lower = even if z == 3 else jnp.logical_not(even)
            change = lambda f, j: jnp.where(lower, own_a[f, j], own_b[f, j])
        else:
            change = lambda f, j: total[f, z, j]
        half = [[base[f, z, j] - (0.5 * step) * change(f, j) for j in range(5)] for f in range(6)]
        kap = [base[KAP, z, j] for j in range(5)]
        for u in half + [kap]:
            edge = pltpu.roll(pltpu.roll(u[3], BW, 1), 1, 0)
            u[0] = jnp.where(last & (row == 6) & (lane < BW), edge, u[0])
            g = jnp.where((row == 0) & (lane < BW), u[0], u[4])
            g = jnp.where((row == 7) & (lane >= LANES - BW), u[3], g)
            u[4] = jnp.where(first & (row == 0) & (lane >= BW), pltpu.roll(g, LANES - BW, 1), g)
        return [state_quantities(*(half[f][j] for f in range(6)), kap[j]) for j in range(5)]

    for z in range(4):
        store_all(q, (z + 1,), own_row(z))
    for edge, change, target in ((edge_a, change_a, jnp.where(even, 5, 0)), (edge_b, change_b, jnp.where(even, 0, 5))):
        found = []
        for j in range(4):
            half = (edge[f, j] - (0.5 * step) * change[f, j] for f in range(6))
            found.append(state_quantities(*half, edge[6, j]))
        store_all(q, (target,), found)

    for key, value in z_face_row(q, 0, 4).items():
        zf[key] = value
    keep = (row < 6) | (arrival[...] > 0.5)
    final[:, 128:160, :] = jnp.zeros((6, 32, LANES), jnp.float32)

    @pl.loop(1, 5, unroll=True)
    def _(z):
        plane = plane_divergence(q, z, 4)
        faces = z_face_row(q, z, 4)
        done = {}
        for (f, j), value in faces.items():
            change = plane[f, j] + (value - zf[f, j])
            done[f, j] = 0.5 * (base[f, z - 1, j] + q[f, z, j]) - (0.25 * step) * change
        for (f, j), value in done.items():
            final[f, pl.ds(4 * j + z - 1, 8, stride=16), :] = jnp.where(keep, value, 0.0)
        for key, value in faces.items():
            zf[key] = value

    fetch.wait()
    start = jnp.where(owner[0] != segment, 32, 0)
    copy = pltpu.make_async_copy(final.at[:, pl.ds(pl.multiple_of(start, 32), 128), :], out, sems.at[1])
    copy.start()
    copy.wait()


def swap(x, partner):
    m, n = lax.axis_size("curve"), lax.axis_size("near")
    route = []
    for c in range(m):
        for i in range(n):
            to_c, to_i = partner(c, i)
            route.append((c * n + i, to_c * n + to_i))
    return lax.ppermute(x, ("curve", "near"), route)


def outer_partner(i, n):
    return ((i + 1) ^ 1) - 1 if 0 < i < n - 1 else n - 1 - i


def rows_view(x):
    lead, cells = x.shape[:-2], x.shape[-1]
    x = x.reshape(lead + (4, cells // LANES, LANES))
    return jnp.swapaxes(x, -3, -2).reshape(lead + (4 * (cells // LANES), LANES))


def kernel(body, name, ins, outs, scratch=(), us=0):
    cost = pl.CostEstimate(flops=int(us * 1e9), bytes_accessed=int(us * 3e6), transcendentals=0) if us else None
    return pl.pallas_call(
        body,
        out_shape=outs,
        in_specs=ins,
        out_specs=jax.tree.map(lambda _: VMEM, outs),
        scratch_shapes=scratch,
        compiler_params=PARAMS,
        cost_estimate=cost,
        name=name,
    )


def local(primitive, conductivity, new_owner):
    m, n = lax.axis_size("curve"), lax.axis_size("near")
    rows = primitive.shape[2] // LANES * 4
    in_hbm = lambda x: pltpu.with_memory_space_constraint(x, pltpu.HBM)
    prim, kappa, new_owner = in_hbm(rows_view(primitive)), in_hbm(rows_view(conductivity)), in_hbm(new_owner)
    hbm = pl.BlockSpec(memory_space=pltpu.HBM)

    side = f32(240, LANES)
    own, msg_c, msg_d, slab, peak = pl.pallas_call(
        load_kernel,
        out_shape=(f32(7, rows, LANES), side, side, f32(7, rows // 2, LANES), f32(1, LANES)),
        in_specs=[hbm] * 3,
        out_specs=(VMEM,) * 5,
        scratch_shapes=[
            pltpu.SMEM(new_owner.shape, jnp.int32),
            pltpu.SemaphoreType.DMA((3,)),
        ],
        compiler_params=PARAMS,
        name="load",
    )(prim, kappa, new_owner)

    rec_c = swap(msg_c, lambda c, i: (c ^ 1, i))
    rec_d = swap(msg_d, lambda c, i: (c, i ^ 1) if c in (0, m - 1) else (outer_partner(c, m), i))
    quantities, sums = f32(NQ, 4, 5, 8, LANES), f32(6, 4, 5, 8, LANES)
    rec_slab = swap(slab, lambda c, i: (c, outer_partner(i, n)))
    peak = kernel(copies_kernel, "copies", [VMEM], f32(m * n, 1, LANES))(peak)
    peak = lax.all_to_all(peak, ("curve", "near"), 0, 0, tiled=True)
    ext, msg_a, msg_b, arrival = kernel(
        spread_kernel,
        "spread",
        [VMEM] * 3,
        (f32(7, 4, 40, LANES), f32(7, 72, LANES), f32(128, LANES), f32(8, LANES)),
        us=COST["spread"],
    )(own, rec_c, rec_d)
    rec_a = swap(msg_a, lambda c, i: (c, i ^ 1))
    rec_b = swap(msg_b, lambda c, i: (c, outer_partner(i, n)))
    q, inner = kernel(inner_kernel, "inner", [VMEM] * 2, (quantities, sums), us=COST["inner"])(ext, rec_slab)
    found = (f32(7, 4, 8, LANES), f32(6, 4, 8, LANES), f32(6, 5, 8, LANES))
    rim = pltpu.VMEM((NQ, 3, 5, 8, LANES), jnp.float32)
    joined = pltpu.VMEM((7, 72, LANES), jnp.float32)
    side_a = kernel(functools.partial(rim_kernel, True), "rim_a", [VMEM] * 3, found, [rim], us=COST["outer"])(
        q, inner, rec_a
    )
    side_b = kernel(functools.partial(rim_kernel, False), "rim_b", [VMEM] * 4, found, [rim, joined], us=COST["outer"])(
        q, inner, rec_slab, rec_b
    )

    out = pl.pallas_call(
        second_kernel,
        out_shape=f32(6, rows + 32, LANES),
        in_specs=[VMEM] * 10 + [hbm],
        out_specs=hbm,
        scratch_shapes=[
            pltpu.VMEM((NQ, 6, 5, 8, LANES), jnp.float32),
            pltpu.VMEM((6, 4, 8, LANES), jnp.float32),
            pltpu.VMEM((6, rows + 64, LANES), jnp.float32),
            pltpu.SMEM(new_owner.shape, jnp.int32),
            pltpu.SemaphoreType.DMA((2,)),
        ],
        compiler_params=PARAMS,
        name="second_section",
    )(q, inner, *side_a, *side_b, arrival, peak, new_owner)
    out = jnp.swapaxes(out.reshape(6, (rows + 32) // 4, 4, LANES), 1, 2)
    return out.reshape(1, 6, 4, (rows + 32) // 4 * LANES)


def solution(mesh):
    in_specs = (P(None, "near", "curve"), P("near", "curve"), P("curve"))
    out_specs = P("curve", None, "near", None)
    return jax.shard_map(local, mesh=mesh, in_specs=in_specs, out_specs=out_specs, check_vma=False)
```

```python
import functools

import jax
import jax.numpy as jnp
from jax import lax
from jax.experimental import pallas as pl
from jax.experimental.pallas import tpu as pltpu
from jax.sharding import PartitionSpec as P

BW = 32
LANES = 128
PLANES = LANES // BW
GAMMA = 1.4
COURANT = 0.8
COST = {"spread": 0.3, "inner": 20, "outer": 20}
NQ = 13
VX, PR, SND, TMP, KAP = 6, 9, 10, 11, 12
VMEM = pl.BlockSpec(memory_space=pltpu.VMEM)
PARAMS = pltpu.CompilerParams(vmem_limit_bytes=24 * 1024 * 1024)


def f32(*shape):
    return jax.ShapeDtypeStruct(shape, jnp.float32)


def lanes_of(shape):
    return lax.broadcasted_iota(jnp.int32, shape, 1)


def rows_of(shape):
    return lax.broadcasted_iota(jnp.int32, shape, 0)


def load_kernel(prim, kappa, new_owner, own, msg_c, msg_d, slab, peak, owner, sems):
    segment = lax.axis_index("curve")
    even, up = segment % 2 == 0, lax.axis_index("near") % 2 == 1
    total = own.shape[1]
    groups = total // 32
    copies = [
        pltpu.make_async_copy(prim, own.at[pl.ds(0, 6)], sems.at[0]),
        pltpu.make_async_copy(kappa, own.at[6], sems.at[1]),
        pltpu.make_async_copy(new_owner, owner, sems.at[2]),
    ]
    for copy in copies:
        copy.start()
    for copy in copies:
        copy.wait()
    speed = top = None
    for g in range(total // 8):
        r = pl.ds(8 * g, 8)
        sound = jnp.sqrt(GAMMA * own[4, r, :] / own[0, r, :])
        s = jnp.abs(own[1, r, :]) + jnp.abs(own[2, r, :]) + jnp.abs(own[3, r, :]) + 3.0 * sound
        speed = s if speed is None else jnp.maximum(speed, s)
        top = own[6, r, :] if top is None else jnp.maximum(top, own[6, r, :])
    speed, top = jnp.max(speed, axis=0, keepdims=True), jnp.max(top, axis=0, keepdims=True)
    halves = [jnp.maximum(v, pltpu.roll(v, LANES // 2, 1)) for v in (speed, top)]
    peak[...] = jnp.where(lanes_of((1, LANES)) < LANES // 2, *halves)
    leaves = jnp.full((2, LANES), (owner[0] != segment).astype(jnp.float32), jnp.float32)
    low_half = lanes_of((1, LANES)) < LANES // 2
    swapped = lambda x: pltpu.roll(x, LANES // 2, 1)
    for msg, box in ((msg_c, jnp.logical_not(even)), (msg_d, even)):
        for f in range(7):
            parts = [own[f, 8 * g : 8 * g + 8, :] for g in range(4)]
            for z in (0, 2):
                first, second = (own[f, k : k + 1, :] for k in (32 + z, 33 + z))
                ahead = jnp.where(low_half, first, swapped(second))
                first, second = (own[f, k : k + 1, :] for k in (total - 4 + z, total - 3 + z))
                parts.append(jnp.where(box, ahead, jnp.where(low_half, swapped(first), second)))
            at = 34 * f
            for part in parts:
                msg[at : at + part.shape[0], :] = part
                at += part.shape[0]
        msg[238:240, :] = leaves
    for f in range(7):
        parts = {}
        for z in range(2):
            for g in range(groups):
                upper, lower = (own[f, pl.ds(k + 32 * g, 8, stride=4), :] for k in (z + 2, z))
                parts[8 * (groups * z + g)] = jnp.where(up, upper, lower)
        for at, value in parts.items():
            slab[f, at : at + 8, :] = value


def copies_kernel(peak, peaks):
    peaks[...] = jnp.broadcast_to(peak[...][None], peaks.shape)


def spread_kernel(own, rec_c, rec_d, ext, msg_a, msg_b, arrival):
    segment, segments = lax.axis_index("curve"), lax.axis_size("curve")
    first, last = segment == 0, segment == segments - 1
    odd = segment % 2 == 1
    up = lax.axis_index("near") % 2 == 0
    groups = own.shape[1] // 32
    shape = (8, LANES)
    lane, row = lanes_of(shape), rows_of(shape)
    spread = lambda x: jnp.broadcast_to(x, shape)
    arrival[...] = jnp.where(last, 0.0, spread(jnp.where(odd, rec_d[238:239, :], rec_c[238:239, :])))
    for f in range(7):
        out = []
        for z in range(4):
            cells = [own[f, pl.ds(z + 32 * g, 8, stride=4), :] for g in range(groups)]
            at = pl.ds(34 * f + z, 8, stride=4)
            box = jnp.where(odd, rec_d[at, :], rec_c[at, :])
            at = pl.ds(34 * f + 32 + z // 2, 1)
            beyond = jnp.where(odd, rec_d[at, :], rec_c[at, :])
            behind = jnp.where(odd, rec_c[at, :], rec_d[at, :])
            if z % 2:
                beyond = pltpu.roll(beyond, LANES // 2, 1)
            else:
                behind = pltpu.roll(behind, LANES // 2, 1)
            beyond, behind = spread(beyond), spread(behind)
            edge = pltpu.roll(spread(cells[-1][7:8]), BW, 1)
            box = jnp.where(last, edge, box)
            start, end = spread(cells[0][0:1]), spread(box[7:8])
            behind = jnp.where(first, pltpu.roll(start, LANES - BW, 1), behind)
            low_side = jnp.where(lane < BW, start, behind)
            high_side = jnp.where(lane >= LANES - BW, end, beyond)
            out.append(cells + [box, jnp.where(row == 7, high_side, low_side)])
        for z in range(4):
            for g, value in enumerate(out[z]):
                ext[f, z, 8 * g : 8 * g + 8, :] = value
        for z in range(2):
            for g in range(groups + 2):
                value = jnp.where(up, out[z + 2][g], out[z][g])
                at = 36 * z + 8 * g
                if g < groups + 1:
                    msg_a[f, at : at + 8, :] = value
                else:
                    msg_a[f, at : at + 1, :] = value[0:1]
                    msg_a[f, at + 1 : at + 2, :] = value[7:8]
            at = 18 * f + 8 * z
            msg_b[at : at + 8, :] = jnp.where(up, out[z][groups], out[z + 2][groups])
        value = jnp.where(up, out[0][groups + 1], out[3][groups + 1])
        msg_b[18 * f + 16 : 18 * f + 17, :] = value[0:1]
        msg_b[18 * f + 17 : 18 * f + 18, :] = value[7:8]
    msg_b[126:128, :] = jnp.zeros((2, LANES), jnp.float32)


def up_x(q, lane):
    w = [pltpu.roll(v, LANES - BW, 1) for v in q[:4]]
    w.append(pltpu.roll(w[0], 7, 0))
    return [jnp.where(lane < LANES - BW, w[j], w[j + 1]) for j in range(4)] + [pltpu.roll(q[4], LANES - BW, 1)]


def up_y(v, low):
    return jnp.where(low == BW - 1, pltpu.roll(v, BW - 1, 1), pltpu.roll(v, LANES - 1, 1))


def down_y(v, low):
    return jnp.where(low == 0, pltpu.roll(v, LANES - BW + 1, 1), pltpu.roll(v, 1, 1))


def face(lower_u, upper_u, lower_f, upper_f, speed, heat):
    out = (lower_f + upper_f) - speed * (upper_u - lower_u)
    return out if heat is None else out - heat


def z_face_row(q, z, slots):
    speed, heat = [], []
    for j in range(slots):
        s0 = jnp.abs(q[VX + 2, z, j]) + q[SND, z, j]
        s1 = jnp.abs(q[VX + 2, z + 1, j]) + q[SND, z + 1, j]
        speed.append(jnp.maximum(s0, s1))
        heat.append((q[KAP, z, j] + q[KAP, z + 1, j]) * (q[TMP, z + 1, j] - q[TMP, z, j]))
    return {
        (f, j): face(
            q[f, z, j],
            q[f, z + 1, j],
            physical(q, f, j, 2, z),
            physical(q, f, j, 2, z + 1),
            speed[j],
            heat[j] if f == 4 else None,
        )
        for f in range(6)
        for j in range(slots)
    }


def physical(q, f, j, k, z):
    if f == 0:
        return q[1 + k, z, j]
    v = q[VX + k, z, j]
    if f == 4:
        return (q[4, z, j] + q[PR, z, j]) * v
    out = q[f, z, j] * v
    return out + q[PR, z, j] if f == 1 + k else out


def plane_divergence(q, z, slots):
    shape = (8, LANES)
    lane, row = lanes_of(shape), rows_of(shape)
    low = lane & (BW - 1)
    ghost = 4
    five = range(5)
    at = lambda i, j: q[i, z, j]
    sx = [jnp.abs(at(VX, j)) + at(SND, j) for j in five]
    sy = [jnp.abs(at(VX + 1, j)) + at(SND, j) for j in range(slots)]
    kx, tx = [at(KAP, j) for j in five], [at(TMP, j) for j in five]
    sxu, kxu, txu = up_x(sx, lane), up_x(kx, lane), up_x(tx, lane)
    syu, kyu, tyu = ([up_y(v, low) for v in vs[:slots]] for vs in (sy, kx, tx))
    ax = [jnp.maximum(v, w) for v, w in zip(sx, sxu, strict=True)]
    ay = [jnp.maximum(v, w) for v, w in zip(sy, syu, strict=True)]
    hx = [(kx[j] + kxu[j]) * (txu[j] - tx[j]) for j in five]
    hy = [(kx[j] + kyu[j]) * (tyu[j] - tx[j]) for j in range(slots)]

    fields = [[at(f, j) for j in five] for f in range(6)]
    fields_x = [up_x(u, lane) for u in fields]
    fields_y = [[up_y(v, low) for v in u[:slots]] for u in fields]

    def neighbours(f):
        if f == 0:
            fx, fux, fy, fuy = fields[1], fields_x[1], fields[2], fields_y[2]
        else:
            fx = [physical(q, f, j, 0, z) for j in five]
            fy = [physical(q, f, j, 1, z) for j in range(slots)]
            fux, fuy = up_x(fx, lane), [up_y(v, low) for v in fy]
        return fields[f], fx, fy, fields_x[f], fux, fields_y[f], fuy

    def sides(f, u, fx, fy, ux, fux, uy, fuy):
        heat = lambda h: h if f == 4 else None
        gx = [face(u[j], ux[j], fx[j], fux[j], ax[j], heat(hx[j])) for j in five]
        gx[3] = jnp.where((lane >= LANES - BW) & (row == 7), gx[ghost], gx[3])
        d = [pltpu.roll(g, BW, 1) for g in gx]
        before = jnp.where(row == 0, d[ghost], pltpu.roll(d[3], 1, 0))
        dx = [jnp.where(lane >= BW, d[j], before if j == 0 else d[j - 1]) for j in range(4)] + [d[ghost]]
        gy = [face(u[j], uy[j], fy[j], fuy[j], ay[j], heat(hy[j])) for j in range(slots)]
        dy = [down_y(g, low) for g in gy]
        return [(gx[j] - dx[j]) + (gy[j] - dy[j]) for j in range(slots)]

    near = [neighbours(f) for f in range(6)]
    part = [sides(f, *near[f]) for f in range(6)]
    return {(f, j): part[f][j] for f in range(6) for j in range(slots)}


def raw_quantities(r, vx, vy, vz, p, s, k):
    t = p / r
    energy = p / (GAMMA - 1.0) + 0.5 * r * (vx * vx + vy * vy + vz * vz)
    return (r, r * vx, r * vy, r * vz, energy, r * s, vx, vy, vz, p, jnp.sqrt(GAMMA * t), t, k)


def state_quantities(r, mx, my, mz, e, s, k):
    inv = 1.0 / r
    vx, vy, vz = mx * inv, my * inv, mz * inv
    p = (GAMMA - 1.0) * (e - 0.5 * (mx * vx + my * vy + mz * vz))
    t = p * inv
    return (r, mx, my, mz, e, s, vx, vy, vz, p, jnp.sqrt(GAMMA * t), t, k)


def store_all(ref, at, values):
    for j, quantities in enumerate(values):
        for i, value in enumerate(quantities):
            ref[(i,) + at + (j,)] = value


def inner_kernel(ext, order, q, total):
    @pl.loop(0, 4, unroll=True)
    def _(z):
        found = []
        for j in range(5):
            rows = pl.ds(j, 8, stride=4) if j < 4 else pl.ds(32, 8)
            found.append(raw_quantities(*(ext[f, z, rows, :] for f in range(7))))
        store_all(q, (z,), found)

    @pl.loop(0, 4, unroll=True)
    def _(z):
        values = plane_divergence(q, z, 5)
        for (f, j), value in values.items():
            total[f, z, j] = value

    @pl.loop(0, 3, unroll=True)
    def _(z):
        faces = z_face_row(q, z, 5)
        lower = {(f, j): total[f, z, j] + value for (f, j), value in faces.items()}
        upper = {(f, j): total[f, z + 1, j] - value for (f, j), value in faces.items()}
        for (f, j), value in lower.items():
            total[f, z, j] = value
        for (f, j), value in upper.items():
            total[f, z + 1, j] = value


def rim_kernel(with_a, q, inner, *refs):
    *received, edge_q, edge_total, own_total, rim = refs[:-1] if not with_a else refs
    even = lax.axis_index("near") % 2 == 0
    above_own = even if with_a else jnp.logical_not(even)
    start, own = jnp.where(above_own, 1, 0), jnp.where(above_own, 3, 0)
    row = rows_of((8, LANES))
    spread = lambda x: jnp.broadcast_to(x, (8, LANES))
    if with_a:
        (rows,) = received
    else:
        rows, (rec_slab, rec_box) = refs[-1], received
        slab = rec_slab.shape[1] // 2
        for f in range(7):
            for z in range(2):
                at, box = 36 * z, 18 * f + 8 * z
                rows[f, at : at + slab, :] = rec_slab[f, slab * z : slab * z + slab, :]
                rows[f, at + slab : at + slab + 8, :] = rec_box[box : box + 8, :]
                rows[f, at + slab + 8 : at + slab + 10, :] = rec_box[18 * f + 16 : 18 * f + 18, :]
    kept = [[q[i, own, j] for i in range(NQ)] for j in range(5)]
    store_all(rim, (jnp.where(above_own, 0, 2),), kept)
    for z in range(2):
        found = []
        for j in range(5):
            if j < 4:
                cells = (rows[f, pl.ds(36 * z + j, 8, stride=4), :] for f in range(7))
            else:
                at = 36 * z + 32
                cells = (
                    jnp.where(row == 7, spread(rows[f, at + 1 : at + 2, :]), spread(rows[f, at : at + 1, :]))
                    for f in range(7)
                )
            found.append(raw_quantities(*cells))
        store_all(rim, (start + z,), found)
    plane = plane_divergence(rim, 1, 4)
    below, above = z_face_row(rim, 0, 5), z_face_row(rim, 1, 5)
    change = {key: jnp.where(above_own, below[key], -above[key]) for key in above}
    done = {(f, j): inner[f, own, j] + value for (f, j), value in change.items()}
    for (f, j), value in plane.items():
        edge_total[f, j] = value + (above[f, j] - below[f, j])
    for (f, j), value in done.items():
        own_total[f, j] = value
    for j in range(4):
        for i, k in enumerate((0, 1, 2, 3, 4, 5, KAP)):
            edge_q[i, j] = rim[k, 1, j]


def second_kernel(
    base, total, edge_a, change_a, own_a, edge_b, change_b, own_b, arrival, peak, new_owner, out, q, zf, final, owner, sems
):
    segment, segments = lax.axis_index("curve"), lax.axis_size("curve")
    shape = (8, LANES)
    lane, row = lanes_of(shape), rows_of(shape)
    first, last = segment == 0, segment == segments - 1
    fetch = pltpu.make_async_copy(new_owner, owner, sems.at[0])
    fetch.start()
    peaks = jnp.max(peak[...], axis=0)
    half_lanes = lanes_of((1, LANES)) < LANES // 2
    both = jnp.broadcast_to(peaks, shape)
    swapped = pltpu.roll(both, LANES // 2, 1)
    speed = jnp.max(jnp.where(lane < LANES // 2, both, 0.0), axis=1, keepdims=True)
    top = jnp.max(jnp.where(lane < LANES // 2, 0.0, both), axis=1, keepdims=True)
    step = jnp.broadcast_to(COURANT / (speed + 6.0 * top), shape)

    even = lax.axis_index("near") % 2 == 0

    def own_row(z):
        if z in (0, 3):
            lower = even if z == 3 else jnp.logical_not(even)
            change = lambda f, j: jnp.where(lower, own_a[f, j], own_b[f, j])
        else:
            change = lambda f, j: total[f, z, j]
        half = [[base[f, z, j] - (0.5 * step) * change(f, j) for j in range(5)] for f in range(6)]
        kap = [base[KAP, z, j] for j in range(5)]
        for u in half + [kap]:
            edge = pltpu.roll(pltpu.roll(u[3], BW, 1), 1, 0)
            u[0] = jnp.where(last & (row == 6) & (lane < BW), edge, u[0])
            g = jnp.where((row == 0) & (lane < BW), u[0], u[4])
            g = jnp.where((row == 7) & (lane >= LANES - BW), u[3], g)
            u[4] = jnp.where(first & (row == 0) & (lane >= BW), pltpu.roll(g, LANES - BW, 1), g)
        return [state_quantities(*(half[f][j] for f in range(6)), kap[j]) for j in range(5)]

    for z in range(4):
        store_all(q, (z + 1,), own_row(z))
    for edge, change, target in ((edge_a, change_a, jnp.where(even, 5, 0)), (edge_b, change_b, jnp.where(even, 0, 5))):
        found = []
        for j in range(4):
            half = (edge[f, j] - (0.5 * step) * change[f, j] for f in range(6))
            found.append(state_quantities(*half, edge[6, j]))
        store_all(q, (target,), found)

    for key, value in z_face_row(q, 0, 4).items():
        zf[key] = value
    keep = (row < 6) | (arrival[...] > 0.5)
    final[:, 128:160, :] = jnp.zeros((6, 32, LANES), jnp.float32)

    @pl.loop(1, 5, unroll=True)
    def _(z):
        plane = plane_divergence(q, z, 4)
        faces = z_face_row(q, z, 4)
        done = {}
        for (f, j), value in faces.items():
            change = plane[f, j] + (value - zf[f, j])
            done[f, j] = 0.5 * (base[f, z - 1, j] + q[f, z, j]) - (0.25 * step) * change
        for (f, j), value in done.items():
            final[f, pl.ds(4 * j + z - 1, 8, stride=16), :] = jnp.where(keep, value, 0.0)
        for key, value in faces.items():
            zf[key] = value

    fetch.wait()
    start = jnp.where(owner[0] != segment, 32, 0)
    copy = pltpu.make_async_copy(final.at[:, pl.ds(pl.multiple_of(start, 32), 128), :], out, sems.at[1])
    copy.start()
    copy.wait()


def swap(x, partner):
    m, n = lax.axis_size("curve"), lax.axis_size("near")
    route = []
    for c in range(m):
        for i in range(n):
            to_c, to_i = partner(c, i)
            route.append((c * n + i, to_c * n + to_i))
    return lax.ppermute(x, ("curve", "near"), route)


def outer_partner(i, n):
    return ((i + 1) ^ 1) - 1 if 0 < i < n - 1 else n - 1 - i


def rows_view(x):
    lead, cells = x.shape[:-2], x.shape[-1]
    x = x.reshape(lead + (4, cells // LANES, LANES))
    return jnp.swapaxes(x, -3, -2).reshape(lead + (4 * (cells // LANES), LANES))


def kernel(body, name, ins, outs, scratch=(), us=0):
    cost = pl.CostEstimate(flops=int(us * 1e9), bytes_accessed=int(us * 3e6), transcendentals=0) if us else None
    return pl.pallas_call(
        body,
        out_shape=outs,
        in_specs=ins,
        out_specs=jax.tree.map(lambda _: VMEM, outs),
        scratch_shapes=scratch,
        compiler_params=PARAMS,
        cost_estimate=cost,
        name=name,
    )


def local(primitive, conductivity, new_owner):
    m, n = lax.axis_size("curve"), lax.axis_size("near")
    rows = primitive.shape[2] // LANES * 4
    in_hbm = lambda x: pltpu.with_memory_space_constraint(x, pltpu.HBM)
    prim, kappa, new_owner = in_hbm(rows_view(primitive)), in_hbm(rows_view(conductivity)), in_hbm(new_owner)
    hbm = pl.BlockSpec(memory_space=pltpu.HBM)

    side = f32(240, LANES)
    own, msg_c, msg_d, slab, peak = pl.pallas_call(
        load_kernel,
        out_shape=(f32(7, rows, LANES), side, side, f32(7, rows // 2, LANES), f32(1, LANES)),
        in_specs=[hbm] * 3,
        out_specs=(VMEM,) * 5,
        scratch_shapes=[
            pltpu.SMEM(new_owner.shape, jnp.int32),
            pltpu.SemaphoreType.DMA((3,)),
        ],
        compiler_params=PARAMS,
        name="load",
    )(prim, kappa, new_owner)

    rec_c = swap(msg_c, lambda c, i: (c ^ 1, i))
    rec_d = swap(msg_d, lambda c, i: (c, i ^ 1) if c in (0, m - 1) else (outer_partner(c, m), i))
    quantities, sums = f32(NQ, 4, 5, 8, LANES), f32(6, 4, 5, 8, LANES)
    rec_slab = swap(slab, lambda c, i: (c, outer_partner(i, n)))
    peak = kernel(copies_kernel, "copies", [VMEM], f32(m * n, 1, LANES))(peak)
    peak = lax.all_to_all(peak, ("curve", "near"), 0, 0, tiled=True)
    ext, msg_a, msg_b, arrival = kernel(
        spread_kernel,
        "spread",
        [VMEM] * 3,
        (f32(7, 4, 40, LANES), f32(7, 72, LANES), f32(128, LANES), f32(8, LANES)),
        us=COST["spread"],
    )(own, rec_c, rec_d)
    rec_a = swap(msg_a, lambda c, i: (c, i ^ 1))
    rec_b = swap(msg_b, lambda c, i: (c, outer_partner(i, n)))
    q, inner = kernel(inner_kernel, "inner", [VMEM] * 2, (quantities, sums), us=COST["inner"])(ext, rec_slab)
    found = (f32(7, 4, 8, LANES), f32(6, 4, 8, LANES), f32(6, 5, 8, LANES))
    rim = pltpu.VMEM((NQ, 3, 5, 8, LANES), jnp.float32)
    joined = pltpu.VMEM((7, 72, LANES), jnp.float32)
    side_a = kernel(functools.partial(rim_kernel, True), "rim_a", [VMEM] * 3, found, [rim], us=COST["outer"])(
        q, inner, rec_a
    )
    side_b = kernel(functools.partial(rim_kernel, False), "rim_b", [VMEM] * 4, found, [rim, joined], us=COST["outer"])(
        q, inner, rec_slab, rec_b
    )

    out = pl.pallas_call(
        second_kernel,
        out_shape=f32(6, rows + 32, LANES),
        in_specs=[VMEM] * 10 + [hbm],
        out_specs=hbm,
        scratch_shapes=[
            pltpu.VMEM((NQ, 6, 5, 8, LANES), jnp.float32),
            pltpu.VMEM((6, 4, 8, LANES), jnp.float32),
            pltpu.VMEM((6, rows + 64, LANES), jnp.float32),
            pltpu.SMEM(new_owner.shape, jnp.int32),
            pltpu.SemaphoreType.DMA((2,)),
        ],
        compiler_params=PARAMS,
        name="second_section",
    )(q, inner, *side_a, *side_b, arrival, peak, new_owner)
    out = jnp.swapaxes(out.reshape(6, (rows + 32) // 4, 4, LANES), 1, 2)
    return out.reshape(1, 6, 4, (rows + 32) // 4 * LANES)


def solution(mesh):
    in_specs = (P(None, "near", "curve"), P("near", "curve"), P("curve"))
    out_specs = P("curve", None, "near", None)
    return jax.shard_map(local, mesh=mesh, in_specs=in_specs, out_specs=out_specs, check_vma=False)
```

```python
import functools

import jax
import jax.numpy as jnp
from jax import lax
from jax.experimental import pallas as pl
from jax.experimental.pallas import tpu as pltpu
from jax.sharding import PartitionSpec as P

BW = 32
LANES = 128
PLANES = LANES // BW
GAMMA = 1.4
COURANT = 0.8
COST = {"spread": 0.3, "inner": 20, "outer": 20}
NQ = 13
VX, PR, SND, TMP, KAP = 6, 9, 10, 11, 12
VMEM = pl.BlockSpec(memory_space=pltpu.VMEM)
PARAMS = pltpu.CompilerParams(vmem_limit_bytes=24 * 1024 * 1024)


def f32(*shape):
    return jax.ShapeDtypeStruct(shape, jnp.float32)


def lanes_of(shape):
    return lax.broadcasted_iota(jnp.int32, shape, 1)


def rows_of(shape):
    return lax.broadcasted_iota(jnp.int32, shape, 0)


def load_kernel(prim, kappa, new_owner, own, msg_c, msg_d, slab, peak, owner, sems):
    segment = lax.axis_index("curve")
    even, up = segment % 2 == 0, lax.axis_index("near") % 2 == 1
    total = own.shape[1]
    groups = total // 32
    copies = [
        *(pltpu.make_async_copy(prim.at[f], own.at[f], sems.at[f]) for f in range(6)),
        pltpu.make_async_copy(kappa, own.at[6], sems.at[6]),
        pltpu.make_async_copy(new_owner, owner, sems.at[7]),
    ]
    for copy in copies:
        copy.start()
    for copy in copies:
        copy.wait()
    speed = top = None
    for g in range(total // 8):
        r = pl.ds(8 * g, 8)
        sound = jnp.sqrt(GAMMA * own[4, r, :] / own[0, r, :])
        s = jnp.abs(own[1, r, :]) + jnp.abs(own[2, r, :]) + jnp.abs(own[3, r, :]) + 3.0 * sound
        speed = s if speed is None else jnp.maximum(speed, s)
        top = own[6, r, :] if top is None else jnp.maximum(top, own[6, r, :])
    speed, top = jnp.max(speed, axis=0, keepdims=True), jnp.max(top, axis=0, keepdims=True)
    halves = [jnp.maximum(v, pltpu.roll(v, LANES // 2, 1)) for v in (speed, top)]
    peak[...] = jnp.where(lanes_of((1, LANES)) < LANES // 2, *halves)
    leaves = jnp.full((2, LANES), (owner[0] != segment).astype(jnp.float32), jnp.float32)
    low_half = lanes_of((1, LANES)) < LANES // 2
    swapped = lambda x: pltpu.roll(x, LANES // 2, 1)
    for msg, box in ((msg_c, jnp.logical_not(even)), (msg_d, even)):
        for f in range(7):
            parts = [own[f, 8 * g : 8 * g + 8, :] for g in range(4)]
            for z in (0, 2):
                first, second = (own[f, k : k + 1, :] for k in (32 + z, 33 + z))
                ahead = jnp.where(low_half, first, swapped(second))
                first, second = (own[f, k : k + 1, :] for k in (total - 4 + z, total - 3 + z))
                parts.append(jnp.where(box, ahead, jnp.where(low_half, swapped(first), second)))
            at = 34 * f
            for part in parts:
                msg[at : at + part.shape[0], :] = part
                at += part.shape[0]
        msg[238:240, :] = leaves
    for f in range(7):
        parts = {}
        for z in range(2):
            for g in range(groups):
                upper, lower = (own[f, pl.ds(k + 32 * g, 8, stride=4), :] for k in (z + 2, z))
                parts[8 * (groups * z + g)] = jnp.where(up, upper, lower)
        for at, value in parts.items():
            slab[f, at : at + 8, :] = value


def copies_kernel(peak, peaks):
    peaks[...] = jnp.broadcast_to(peak[...][None], peaks.shape)


def spread_kernel(own, rec_c, rec_d, ext, msg_a, msg_b, arrival):
    segment, segments = lax.axis_index("curve"), lax.axis_size("curve")
    first, last = segment == 0, segment == segments - 1
    odd = segment % 2 == 1
    up = lax.axis_index("near") % 2 == 0
    groups = own.shape[1] // 32
    shape = (8, LANES)
    lane, row = lanes_of(shape), rows_of(shape)
    spread = lambda x: jnp.broadcast_to(x, shape)
    arrival[...] = jnp.where(last, 0.0, spread(jnp.where(odd, rec_d[238:239, :], rec_c[238:239, :])))
    for f in range(7):
        out = []
        for z in range(4):
            cells = [own[f, pl.ds(z + 32 * g, 8, stride=4), :] for g in range(groups)]
            at = pl.ds(34 * f + z, 8, stride=4)
            box = jnp.where(odd, rec_d[at, :], rec_c[at, :])
            at = pl.ds(34 * f + 32 + z // 2, 1)
            beyond = jnp.where(odd, rec_d[at, :], rec_c[at, :])
            behind = jnp.where(odd, rec_c[at, :], rec_d[at, :])
            if z % 2:
                beyond = pltpu.roll(beyond, LANES // 2, 1)
            else:
                behind = pltpu.roll(behind, LANES // 2, 1)
            beyond, behind = spread(beyond), spread(behind)
            edge = pltpu.roll(spread(cells[-1][7:8]), BW, 1)
            box = jnp.where(last, edge, box)
            start, end = spread(cells[0][0:1]), spread(box[7:8])
            behind = jnp.where(first, pltpu.roll(start, LANES - BW, 1), behind)
            low_side = jnp.where(lane < BW, start, behind)
            high_side = jnp.where(lane >= LANES - BW, end, beyond)
            out.append(cells + [box, jnp.where(row == 7, high_side, low_side)])
        for z in range(4):
            for g, value in enumerate(out[z]):
                ext[f, z, 8 * g : 8 * g + 8, :] = value
        for z in range(2):
            for g in range(groups + 2):
                value = jnp.where(up, out[z + 2][g], out[z][g])
                at = 36 * z + 8 * g
                if g < groups + 1:
                    msg_a[f, at : at + 8, :] = value
                else:
                    msg_a[f, at : at + 1, :] = value[0:1]
                    msg_a[f, at + 1 : at + 2, :] = value[7:8]
            at = 18 * f + 8 * z
            msg_b[at : at + 8, :] = jnp.where(up, out[z][groups], out[z + 2][groups])
        value = jnp.where(up, out[0][groups + 1], out[3][groups + 1])
        msg_b[18 * f + 16 : 18 * f + 17, :] = value[0:1]
        msg_b[18 * f + 17 : 18 * f + 18, :] = value[7:8]
    msg_b[126:128, :] = jnp.zeros((2, LANES), jnp.float32)


def up_x(q, lane):
    w = [pltpu.roll(v, LANES - BW, 1) for v in q[:4]]
    w.append(pltpu.roll(w[0], 7, 0))
    return [jnp.where(lane < LANES - BW, w[j], w[j + 1]) for j in range(4)] + [pltpu.roll(q[4], LANES - BW, 1)]


def up_y(v, low):
    return jnp.where(low == BW - 1, pltpu.roll(v, BW - 1, 1), pltpu.roll(v, LANES - 1, 1))


def down_y(v, low):
    return jnp.where(low == 0, pltpu.roll(v, LANES - BW + 1, 1), pltpu.roll(v, 1, 1))


def face(lower_u, upper_u, lower_f, upper_f, speed, heat):
    out = (lower_f + upper_f) - speed * (upper_u - lower_u)
    return out if heat is None else out - heat


def z_face_row(q, z, slots):
    speed, heat = [], []
    for j in range(slots):
        s0 = jnp.abs(q[VX + 2, z, j]) + q[SND, z, j]
        s1 = jnp.abs(q[VX + 2, z + 1, j]) + q[SND, z + 1, j]
        speed.append(jnp.maximum(s0, s1))
        heat.append((q[KAP, z, j] + q[KAP, z + 1, j]) * (q[TMP, z + 1, j] - q[TMP, z, j]))
    return {
        (f, j): face(
            q[f, z, j],
            q[f, z + 1, j],
            physical(q, f, j, 2, z),
            physical(q, f, j, 2, z + 1),
            speed[j],
            heat[j] if f == 4 else None,
        )
        for f in range(6)
        for j in range(slots)
    }


def physical(q, f, j, k, z):
    if f == 0:
        return q[1 + k, z, j]
    v = q[VX + k, z, j]
    if f == 4:
        return (q[4, z, j] + q[PR, z, j]) * v
    out = q[f, z, j] * v
    return out + q[PR, z, j] if f == 1 + k else out


def plane_divergence(q, z, slots):
    shape = (8, LANES)
    lane, row = lanes_of(shape), rows_of(shape)
    low = lane & (BW - 1)
    ghost = 4
    five = range(5)
    at = lambda i, j: q[i, z, j]
    sx = [jnp.abs(at(VX, j)) + at(SND, j) for j in five]
    sy = [jnp.abs(at(VX + 1, j)) + at(SND, j) for j in range(slots)]
    kx, tx = [at(KAP, j) for j in five], [at(TMP, j) for j in five]
    sxu, kxu, txu = up_x(sx, lane), up_x(kx, lane), up_x(tx, lane)
    syu, kyu, tyu = ([up_y(v, low) for v in vs[:slots]] for vs in (sy, kx, tx))
    ax = [jnp.maximum(v, w) for v, w in zip(sx, sxu, strict=True)]
    ay = [jnp.maximum(v, w) for v, w in zip(sy, syu, strict=True)]
    hx = [(kx[j] + kxu[j]) * (txu[j] - tx[j]) for j in five]
    hy = [(kx[j] + kyu[j]) * (tyu[j] - tx[j]) for j in range(slots)]

    fields = [[at(f, j) for j in five] for f in range(6)]
    fields_x = [up_x(u, lane) for u in fields]
    fields_y = [[up_y(v, low) for v in u[:slots]] for u in fields]

    def neighbours(f):
        if f == 0:
            fx, fux, fy, fuy = fields[1], fields_x[1], fields[2], fields_y[2]
        else:
            fx = [physical(q, f, j, 0, z) for j in five]
            fy = [physical(q, f, j, 1, z) for j in range(slots)]
            fux, fuy = up_x(fx, lane), [up_y(v, low) for v in fy]
        return fields[f], fx, fy, fields_x[f], fux, fields_y[f], fuy

    def sides(f, u, fx, fy, ux, fux, uy, fuy):
        heat = lambda h: h if f == 4 else None
        gx = [face(u[j], ux[j], fx[j], fux[j], ax[j], heat(hx[j])) for j in five]
        gx[3] = jnp.where((lane >= LANES - BW) & (row == 7), gx[ghost], gx[3])
        d = [pltpu.roll(g, BW, 1) for g in gx]
        before = jnp.where(row == 0, d[ghost], pltpu.roll(d[3], 1, 0))
        dx = [jnp.where(lane >= BW, d[j], before if j == 0 else d[j - 1]) for j in range(4)] + [d[ghost]]
        gy = [face(u[j], uy[j], fy[j], fuy[j], ay[j], heat(hy[j])) for j in range(slots)]
        dy = [down_y(g, low) for g in gy]
        return [(gx[j] - dx[j]) + (gy[j] - dy[j]) for j in range(slots)]

    near = [neighbours(f) for f in range(6)]
    part = [sides(f, *near[f]) for f in range(6)]
    return {(f, j): part[f][j] for f in range(6) for j in range(slots)}


def raw_quantities(r, vx, vy, vz, p, s, k):
    t = p / r
    energy = p / (GAMMA - 1.0) + 0.5 * r * (vx * vx + vy * vy + vz * vz)
    return (r, r * vx, r * vy, r * vz, energy, r * s, vx, vy, vz, p, jnp.sqrt(GAMMA * t), t, k)


def state_quantities(r, mx, my, mz, e, s, k):
    inv = 1.0 / r
    vx, vy, vz = mx * inv, my * inv, mz * inv
    p = (GAMMA - 1.0) * (e - 0.5 * (mx * vx + my * vy + mz * vz))
    t = p * inv
    return (r, mx, my, mz, e, s, vx, vy, vz, p, jnp.sqrt(GAMMA * t), t, k)


def store_all(ref, at, values):
    for j, quantities in enumerate(values):
        for i, value in enumerate(quantities):
            ref[(i,) + at + (j,)] = value


def inner_kernel(ext, order, q, total):
    @pl.loop(0, 4, unroll=True)
    def _(z):
        found = []
        for j in range(5):
            rows = pl.ds(j, 8, stride=4) if j < 4 else pl.ds(32, 8)
            found.append(raw_quantities(*(ext[f, z, rows, :] for f in range(7))))
        store_all(q, (z,), found)

    @pl.loop(0, 4, unroll=True)
    def _(z):
        values = plane_divergence(q, z, 5)
        for (f, j), value in values.items():
            total[f, z, j] = value

    @pl.loop(0, 3, unroll=True)
    def _(z):
        faces = z_face_row(q, z, 5)
        lower = {(f, j): total[f, z, j] + value for (f, j), value in faces.items()}
        upper = {(f, j): total[f, z + 1, j] - value for (f, j), value in faces.items()}
        for (f, j), value in lower.items():
            total[f, z, j] = value
        for (f, j), value in upper.items():
            total[f, z + 1, j] = value


def rim_kernel(with_a, q, inner, *refs):
    *received, edge_q, edge_total, own_total, rim = refs[:-1] if not with_a else refs
    even = lax.axis_index("near") % 2 == 0
    above_own = even if with_a else jnp.logical_not(even)
    start, own = jnp.where(above_own, 1, 0), jnp.where(above_own, 3, 0)
    row = rows_of((8, LANES))
    spread = lambda x: jnp.broadcast_to(x, (8, LANES))
    if with_a:
        (rows,) = received
    else:
        rows, (rec_slab, rec_box) = refs[-1], received
        slab = rec_slab.shape[1] // 2
        for f in range(7):
            for z in range(2):
                at, box = 36 * z, 18 * f + 8 * z
                rows[f, at : at + slab, :] = rec_slab[f, slab * z : slab * z + slab, :]
                rows[f, at + slab : at + slab + 8, :] = rec_box[box : box + 8, :]
                rows[f, at + slab + 8 : at + slab + 10, :] = rec_box[18 * f + 16 : 18 * f + 18, :]
    kept = [[q[i, own, j] for i in range(NQ)] for j in range(5)]
    store_all(rim, (jnp.where(above_own, 0, 2),), kept)
    for z in range(2):
        found = []
        for j in range(5):
            if j < 4:
                cells = (rows[f, pl.ds(36 * z + j, 8, stride=4), :] for f in range(7))
            else:
                at = 36 * z + 32
                cells = (
                    jnp.where(row == 7, spread(rows[f, at + 1 : at + 2, :]), spread(rows[f, at : at + 1, :]))
                    for f in range(7)
                )
            found.append(raw_quantities(*cells))
        store_all(rim, (start + z,), found)
    plane = plane_divergence(rim, 1, 4)
    below, above = z_face_row(rim, 0, 5), z_face_row(rim, 1, 5)
    change = {key: jnp.where(above_own, below[key], -above[key]) for key in above}
    done = {(f, j): inner[f, own, j] + value for (f, j), value in change.items()}
    for (f, j), value in plane.items():
        edge_total[f, j] = value + (above[f, j] - below[f, j])
    for (f, j), value in done.items():
        own_total[f, j] = value
    for j in range(4):
        for i, k in enumerate((0, 1, 2, 3, 4, 5, KAP)):
            edge_q[i, j] = rim[k, 1, j]


def second_kernel(
    base, total, edge_a, change_a, own_a, edge_b, change_b, own_b, arrival, peak, new_owner, out, q, zf, final, owner, sems
):
    segment, segments = lax.axis_index("curve"), lax.axis_size("curve")
    shape = (8, LANES)
    lane, row = lanes_of(shape), rows_of(shape)
    first, last = segment == 0, segment == segments - 1
    fetch = pltpu.make_async_copy(new_owner, owner, sems.at[0])
    fetch.start()
    peaks = jnp.max(peak[...], axis=0)
    half_lanes = lanes_of((1, LANES)) < LANES // 2
    both = jnp.broadcast_to(peaks, shape)
    swapped = pltpu.roll(both, LANES // 2, 1)
    speed = jnp.max(jnp.where(lane < LANES // 2, both, 0.0), axis=1, keepdims=True)
    top = jnp.max(jnp.where(lane < LANES // 2, 0.0, both), axis=1, keepdims=True)
    step = jnp.broadcast_to(COURANT / (speed + 6.0 * top), shape)

    even = lax.axis_index("near") % 2 == 0

    def own_row(z):
        if z in (0, 3):
            lower = even if z == 3 else jnp.logical_not(even)
            change = lambda f, j: jnp.where(lower, own_a[f, j], own_b[f, j])
        else:
            change = lambda f, j: total[f, z, j]
        half = [[base[f, z, j] - (0.5 * step) * change(f, j) for j in range(5)] for f in range(6)]
        kap = [base[KAP, z, j] for j in range(5)]
        for u in half + [kap]:
            edge = pltpu.roll(pltpu.roll(u[3], BW, 1), 1, 0)
            u[0] = jnp.where(last & (row == 6) & (lane < BW), edge, u[0])
            g = jnp.where((row == 0) & (lane < BW), u[0], u[4])
            g = jnp.where((row == 7) & (lane >= LANES - BW), u[3], g)
            u[4] = jnp.where(first & (row == 0) & (lane >= BW), pltpu.roll(g, LANES - BW, 1), g)
        return [state_quantities(*(half[f][j] for f in range(6)), kap[j]) for j in range(5)]

    for z in range(4):
        store_all(q, (z + 1,), own_row(z))
    for edge, change, target in ((edge_a, change_a, jnp.where(even, 5, 0)), (edge_b, change_b, jnp.where(even, 0, 5))):
        found = []
        for j in range(4):
            half = (edge[f, j] - (0.5 * step) * change[f, j] for f in range(6))
            found.append(state_quantities(*half, edge[6, j]))
        store_all(q, (target,), found)

    for key, value in z_face_row(q, 0, 4).items():
        zf[key] = value
    keep = (row < 6) | (arrival[...] > 0.5)
    final[:, 128:160, :] = jnp.zeros((6, 32, LANES), jnp.float32)

    @pl.loop(1, 5, unroll=True)
    def _(z):
        plane = plane_divergence(q, z, 4)
        faces = z_face_row(q, z, 4)
        done = {}
        for (f, j), value in faces.items():
            change = plane[f, j] + (value - zf[f, j])
            done[f, j] = 0.5 * (base[f, z - 1, j] + q[f, z, j]) - (0.25 * step) * change
        for (f, j), value in done.items():
            final[f, pl.ds(4 * j + z - 1, 8, stride=16), :] = jnp.where(keep, value, 0.0)
        for key, value in faces.items():
            zf[key] = value

    fetch.wait()
    start = jnp.where(owner[0] != segment, 32, 0)
    copy = pltpu.make_async_copy(final.at[:, pl.ds(pl.multiple_of(start, 32), 128), :], out, sems.at[1])
    copy.start()
    copy.wait()


def swap(x, partner):
    m, n = lax.axis_size("curve"), lax.axis_size("near")
    route = []
    for c in range(m):
        for i in range(n):
            to_c, to_i = partner(c, i)
            route.append((c * n + i, to_c * n + to_i))
    return lax.ppermute(x, ("curve", "near"), route)


def outer_partner(i, n):
    return ((i + 1) ^ 1) - 1 if 0 < i < n - 1 else n - 1 - i


def rows_view(x):
    lead, cells = x.shape[:-2], x.shape[-1]
    x = x.reshape(lead + (4, cells // LANES, LANES))
    return jnp.swapaxes(x, -3, -2).reshape(lead + (4 * (cells // LANES), LANES))


def kernel(body, name, ins, outs, scratch=(), us=0):
    cost = pl.CostEstimate(flops=int(us * 1e9), bytes_accessed=int(us * 3e6), transcendentals=0) if us else None
    return pl.pallas_call(
        body,
        out_shape=outs,
        in_specs=ins,
        out_specs=jax.tree.map(lambda _: VMEM, outs),
        scratch_shapes=scratch,
        compiler_params=PARAMS,
        cost_estimate=cost,
        name=name,
    )


def local(primitive, conductivity, new_owner):
    m, n = lax.axis_size("curve"), lax.axis_size("near")
    rows = primitive.shape[2] // LANES * 4
    in_hbm = lambda x: pltpu.with_memory_space_constraint(x, pltpu.HBM)
    prim, kappa, new_owner = in_hbm(rows_view(primitive)), in_hbm(rows_view(conductivity)), in_hbm(new_owner)
    hbm = pl.BlockSpec(memory_space=pltpu.HBM)

    side = f32(240, LANES)
    own, msg_c, msg_d, slab, peak = pl.pallas_call(
        load_kernel,
        out_shape=(f32(7, rows, LANES), side, side, f32(7, rows // 2, LANES), f32(1, LANES)),
        in_specs=[hbm] * 3,
        out_specs=(VMEM,) * 5,
        scratch_shapes=[
            pltpu.SMEM(new_owner.shape, jnp.int32),
            pltpu.SemaphoreType.DMA((8,)),
        ],
        compiler_params=PARAMS,
        name="load",
    )(prim, kappa, new_owner)

    rec_c = swap(msg_c, lambda c, i: (c ^ 1, i))
    rec_d = swap(msg_d, lambda c, i: (c, i ^ 1) if c in (0, m - 1) else (outer_partner(c, m), i))
    quantities, sums = f32(NQ, 4, 5, 8, LANES), f32(6, 4, 5, 8, LANES)
    rec_slab = swap(slab, lambda c, i: (c, outer_partner(i, n)))
    peak = kernel(copies_kernel, "copies", [VMEM], f32(m * n, 1, LANES))(peak)
    peak = lax.all_to_all(peak, ("curve", "near"), 0, 0, tiled=True)
    ext, msg_a, msg_b, arrival = kernel(
        spread_kernel,
        "spread",
        [VMEM] * 3,
        (f32(7, 4, 40, LANES), f32(7, 72, LANES), f32(128, LANES), f32(8, LANES)),
        us=COST["spread"],
    )(own, rec_c, rec_d)
    rec_a = swap(msg_a, lambda c, i: (c, i ^ 1))
    rec_b = swap(msg_b, lambda c, i: (c, outer_partner(i, n)))
    q, inner = kernel(inner_kernel, "inner", [VMEM] * 2, (quantities, sums), us=COST["inner"])(ext, rec_slab)
    found = (f32(7, 4, 8, LANES), f32(6, 4, 8, LANES), f32(6, 5, 8, LANES))
    rim = pltpu.VMEM((NQ, 3, 5, 8, LANES), jnp.float32)
    joined = pltpu.VMEM((7, 72, LANES), jnp.float32)
    side_a = kernel(functools.partial(rim_kernel, True), "rim_a", [VMEM] * 3, found, [rim], us=COST["outer"])(
        q, inner, rec_a
    )
    side_b = kernel(functools.partial(rim_kernel, False), "rim_b", [VMEM] * 4, found, [rim, joined], us=COST["outer"])(
        q, inner, rec_slab, rec_b
    )

    out = pl.pallas_call(
        second_kernel,
        out_shape=f32(6, rows + 32, LANES),
        in_specs=[VMEM] * 10 + [hbm],
        out_specs=hbm,
        scratch_shapes=[
            pltpu.VMEM((NQ, 6, 5, 8, LANES), jnp.float32),
            pltpu.VMEM((6, 4, 8, LANES), jnp.float32),
            pltpu.VMEM((6, rows + 64, LANES), jnp.float32),
            pltpu.SMEM(new_owner.shape, jnp.int32),
            pltpu.SemaphoreType.DMA((2,)),
        ],
        compiler_params=PARAMS,
        name="second_section",
    )(q, inner, *side_a, *side_b, arrival, peak, new_owner)
    out = jnp.swapaxes(out.reshape(6, (rows + 32) // 4, 4, LANES), 1, 2)
    return out.reshape(1, 6, 4, (rows + 32) // 4 * LANES)


def solution(mesh):
    in_specs = (P(None, "near", "curve"), P("near", "curve"), P("curve"))
    out_specs = P("curve", None, "near", None)
    return jax.shard_map(local, mesh=mesh, in_specs=in_specs, out_specs=out_specs, check_vma=False)
```
